256 devices in a mesh: ctx: 16 (over y, x_lo, core), head: 8 (over z), grp: 2 (over x_hi).
Axes of the slice: x: 4 (x_hi: 2, x_lo: 2; x = x_hi * 2 + x_lo), y: 4, z: 8, core: 2. Of those that a mesh axis runs over, the one named last changes fastest.
Arguments:
- queries: bfloat16 [8192, 8192], P(('ctx', 'grp'), 'head'), may hold values from -18 to 18
- answer_kv: bfloat16 [8192, 8, 256], P(('ctx', 'grp'), 'head'), may hold values from -8 to 8
- prompt_kv: bfloat16 [2, 8192, 8, 256], P('grp', 'ctx', 'head'), may hold values from -8 to 8
- block_prompt: int32 [64, 1], P(('ctx', 'grp')), may hold values from 0 to 1; in each aligned block of 2 rows (0 to 1, 2 to 3, ...) at most 2 rows name the same one
- answer_len: int32 [64], P(('ctx', 'grp')), may hold values from 1 to 128, 5120 in all
Outputs:
- attended: bfloat16 [8192, 8192], P(('ctx', 'grp'), 'head')
The draws below stay inside these ranges and needn't reach their ends.
Inputs may be any that keep to these rules, and one draw needn't show every extreme that they name: `block_prompt`: of the 2 blocks that one index of ctx and grp holds (aligned blocks of rows), at most 2 name any one prompt.
All inputs are finite; a program needn't handle non-finite values. No bound on the sum of `answer_len` on one device may be relied on, other than what follows from the above.
Results may differ from the reference program's by a relative error of at most 0.0055.
Values may be sent and summed in bfloat16 or wider, within the bound.
No kernel may reach another device: no remote copies, remote signals or barrier semaphores. Data moves between devices by JAX's collectives and lax.ppermute only.
A program may use at most 256 MiB of HBM per device.

```python
import math
import jax
import jax.numpy as jnp
import numpy as np
from jax import lax

H = 64
KVH = 8
HD = 128
BROWS = 128
BLK_DEV = 2
CAP = 2
GROUPS = 2
PROMPT = 8192
BLOCKS = 64
ROWS = 8192


def draw_queries(key, part):
    key = jax.random.fold_in(key, 11)
    first = jax.random.fold_in(key, 0)
    shape = (ROWS, H * HD)
    values = jnp.clip(jax.random.normal(first, shape, jnp.float32) * 1.6, -8.0, 8.0)
    return values.astype(jnp.bfloat16)


def draw_prompt_kv(key, part):
    key = jax.random.fold_in(key, 12)
    first, second = jax.random.split(key, 2)
    shape = (GROUPS, PROMPT, KVH, HD)
    keys = jnp.clip(jax.random.normal(first, shape, jnp.float32) * 1.6, -8.0, 8.0)
    values = jnp.clip(jax.random.normal(second, shape, jnp.float32), -8.0, 8.0)
    return jnp.concatenate([keys, values], axis=-1).astype(jnp.bfloat16)


def block_scale(rng, shape, cuts, least, largest):
    def one(dim, shards_of):
        steps = jax.random.uniform(jax.random.fold_in(jax.random.fold_in(rng, 6), dim), (shards_of,), jnp.float32, least / len(cuts), largest / len(cuts))
        return jnp.repeat(jnp.exp(steps), shape[dim] // shards_of).reshape((-1,) + (1,) * (len(shape) - dim - 1))

    gain = one(*cuts[0])
    for cut in cuts[1:]:
        gain = gain * one(*cut)
    return gain


def profile(number_of, total, limit, skew):
    portions = [(1 << 20) // math.isqrt(rank ** skew) + 1 for rank in range(2, number_of + 1)]
    surplus, holding = total - limit - (number_of - 1), [1] * (number_of - 1)
    while surplus > 0:
        free = [i for i in range(number_of - 1) if holding[i] < limit]
        whole, budget = sum([portions[i] for i in free]), surplus
        for i in free:
            more = min(limit - holding[i], max(1, budget * portions[i] // whole), surplus)
            holding[i] = holding[i] + more
            surplus = surplus - more
    return np.array([limit] + holding)


def uneven_parts(key, amount, total, limit, slope):
    if amount == 2:
        one = jax.random.randint(key, (), max(1, total - limit), min(limit, total - 1) + 1)
        return jnp.stack([one, total - one])
    tallies = jnp.asarray(profile(amount, total, limit, slope), jnp.int32)
    twos = (amount - 1) // 2
    giver, receiver = tallies[1:1 + 2 * twos:2], tallies[2:2 + 2 * twos:2]
    margin = jnp.minimum(giver - 1, limit - receiver)
    passed = jax.random.randint(jax.random.fold_in(key, 1), (twos,), 0, 1 << 20) % (margin + 1)
    tallies = tallies.at[1:1 + 2 * twos:2].set(giver - passed).at[2:2 + 2 * twos:2].set(receiver + passed)
    return tallies[jax.random.permutation(jax.random.fold_in(key, 2), amount)]


def assign_block(rng, own, number, rows, count, top, bound, lean):
    ranking = jax.random.permutation(rng, count)
    crowded, common = load_shares(count, rows * top, bound, lean, True), load_shares(count, rows * top, bound, lean, False)
    places = jnp.arange(count)

    def named(sizes, offset_by):
        used = int((sizes > 0).sum())
        fixed = max(1, used // 4)
        moved = fixed + (places - fixed + offset_by * (used - fixed)) % max(1, count - fixed)
        return jnp.zeros((count,), jnp.int32).at[ranking[jnp.where(places < fixed, places, moved)]].set(jnp.asarray(sizes, jnp.int32))

    sizes = jnp.where(number % 4 == 0, named(crowded, number // 4), named(common, number - number // 4 - 1))
    mixed = jax.random.permutation(jax.random.fold_in(own, 3), count)
    giver, sink = mixed[0:count // 2 * 2:2], mixed[1:count // 2 * 2:2]
    margin = jnp.minimum(sizes[giver] - 1, bound - sizes[sink]) // 2
    margin = jnp.where((giver == ranking[0]) | (sink == ranking[0]) | (sizes[sink] == 0), 0, jnp.maximum(margin, 0))
    moved = jax.random.randint(jax.random.fold_in(own, 4), (count // 2,), 0, 1 << 20) % (margin + 1)
    sizes = sizes.at[giver].add(-moved).at[sink].add(moved)
    labels = jnp.searchsorted(jnp.cumsum(sizes), jnp.arange(rows * top), side="right").astype(jnp.int32)
    grid = labels.reshape(top, rows).T
    grid = grid[jax.random.permutation(jax.random.fold_in(own, 1), rows)]
    offset_by = jax.random.randint(jax.random.fold_in(own, 2), (rows, 1), 0, top)
    return jnp.take_along_axis(grid, (jnp.arange(top)[None, :] + offset_by) % top, axis=1)


def load_shares(count, total, bound, slope, full):
    weights = [(1 << 20) // math.isqrt(standing ** slope) + 1 for standing in range(1, count + 1)]
    largest = bound if full else min(bound, max(-(-total // count), total * weights[0] // sum(weights)))
    least = 1 if total - largest >= count - 1 else 0
    counts, spare = [largest] + [least] * (count - 1), total - largest - least * (count - 1)
    while spare > 0:
        candidates = [i for i in range(1, count) if counts[i] < largest] or [i for i in range(1, count) if counts[i] < bound]
        pool, left = sum([weights[i] for i in candidates]), spare
        for i in candidates:
            addition = min(bound - counts[i], max(1, left * weights[i] // pool), spare)
            counts[i] = counts[i] + addition
            spare = spare - addition
    return np.array(counts)


def noise(own_key, dims, deviation, reach, cuts=(), kind=jnp.bfloat16):
    gain = block_scale(own_key, dims, cuts, -0.22, 0.18) if cuts else 1.0
    values = jax.random.normal(own_key, dims, jnp.float32) * deviation * gain
    return jnp.minimum(jnp.maximum(values, -reach), reach).astype(kind)


def setup_inputs(seed: int = 0) -> dict:
    seeds = jax.random.split(jax.random.key(seed), 6)
    queries = draw_queries(jax.random.fold_in(seeds[5], 71), 0)
    answer_kv = noise(seeds[1], (ROWS, KVH, 2 * HD), 1.8, 8.0, ((0, 32), (1, 8)))
    prompt_kv = draw_prompt_kv(jax.random.fold_in(seeds[5], 71), 0)
    block_prompt_keys = jax.random.split(jax.random.fold_in(seeds[3], 1), BLOCKS // BLK_DEV)
    block_prompt_turns = jax.random.permutation(jax.random.fold_in(seeds[3], 3), BLOCKS // BLK_DEV)
    block_prompt = jax.vmap(lambda own, number: assign_block(jax.random.fold_in(seeds[3], 2), own, number, BLK_DEV, GROUPS, 1, CAP, 2))(block_prompt_keys, block_prompt_turns).reshape((BLOCKS, 1))
    answer_len = uneven_parts(seeds[4], BLOCKS, BLOCKS * BROWS * 5 // 8, BROWS, 1).astype(jnp.int32)
    return {"queries": queries, "answer_kv": answer_kv, "prompt_kv": prompt_kv, "block_prompt": block_prompt, "answer_len": answer_len}


def rounded(weights):
    held = lax.optimization_barrier(weights.astype(jnp.bfloat16))
    return held.astype(jnp.float32)


def reference(queries, answer_kv, prompt_kv, block_prompt, answer_len):
    group = H // KVH
    scale = 1.0 / (HD ** 0.5)
    q_all = queries.reshape(BLOCKS, BROWS, KVH, group, HD)
    kv_all = answer_kv.reshape(BLOCKS, BROWS, KVH, 2 * HD)
    positions = jnp.arange(BROWS, dtype=jnp.int32)
    causal = positions[:, None] >= positions[None, :]

    def one_block(items):
        q_block, kv_block, target, length = items
        prompt = lax.dynamic_index_in_dim(prompt_kv, target.astype(jnp.int32), 0, keepdims=False)
        q_float = q_block.astype(jnp.float32)
        scores = jnp.einsum("qkgd,pkd->qkgp", q_float, prompt[..., :HD].astype(jnp.float32)) * scale
        own_scores = jnp.einsum("qkgd,jkd->qkgj", q_float, kv_block[..., :HD].astype(jnp.float32)) * scale
        mask = causal[:, None, None, :]
        own_scores = jnp.where(mask, own_scores, -jnp.inf)
        peak = jnp.maximum(jnp.max(scores, axis=-1), jnp.max(own_scores, axis=-1))
        weights = jnp.exp(scores - peak[..., None])
        own_weights = jnp.where(mask, jnp.exp(own_scores - peak[..., None]), 0.0)
        total = jnp.sum(weights, axis=-1) + jnp.sum(own_weights, axis=-1)
        blended = jnp.einsum("qkgp,pkd->qkgd", rounded(weights), prompt[..., HD:].astype(jnp.float32), precision=lax.Precision.HIGHEST)
        blended = blended + jnp.einsum("qkgj,jkd->qkgd", rounded(own_weights), kv_block[..., HD:].astype(jnp.float32), precision=lax.Precision.HIGHEST)
        blended = blended / total[..., None]
        live = positions < length
        blended = jnp.where(live[:, None, None, None], blended, 0.0)
        return blended.reshape(BROWS, H * HD).astype(jnp.bfloat16)

    result = lax.map(one_block, (q_all, kv_all, block_prompt[:, 0], answer_len))
    return result.reshape(ROWS, H * HD)
```

```python
import functools

import jax
import jax.numpy as jnp
import numpy as np
from jax import lax
from jax.experimental import pallas as pl
from jax.experimental.pallas import tpu as pltpu
from jax.sharding import PartitionSpec as P

HD = 128
BROWS = 128
HEADS = 8
UNIT = 256
GROUP = 16
LIST = 48
STATE_ROWS = 40 * GROUP * HEADS
SCALE = float(np.log2(np.e) / np.sqrt(HD))
LOW = -1e30
VMEM = pl.BlockSpec(memory_space=pltpu.VMEM)
SMEM = pl.BlockSpec(memory_space=pltpu.SMEM)
AXES = ("ctx", "grp")

SWAPS = {
    "xe": lambda x, y: (x ^ 1, y),
    "xo": lambda x, y: (3 - x, y),
    "ye": lambda x, y: (x, y ^ 1),
    "yo": lambda x, y: (x, 3 - y),
}
ROUTES = (
    (("xo", "xe", "ye", "yo"), ("yo", "xo", "xe", "ye")),
    (("ye", "yo", "xo", "xe"), ("xe", "ye", "yo", "xo")),
)


def index_of(x, y, core):
    return ((y * 2 + x % 2) * 2 + core) * 2 + x // 2


def chip_swap(chain, step):
    pairs = []
    for x in range(4):
        for y in range(4):
            for core in range(2):
                nx, ny = SWAPS[ROUTES[chain][core][step]](x, y)
                pairs.append((index_of(x, y, core), index_of(nx, ny, core)))
    return pairs


def core_swap():
    return [(index_of(x, y, c), index_of(x, y, 1 - c)) for x in range(4) for y in range(4) for c in range(2)]


def scaled(q):
    wide = q.astype(jnp.float32) * SCALE
    high = wide.astype(jnp.bfloat16)
    low = (wide - high.astype(jnp.float32)).astype(jnp.bfloat16)
    return jnp.concatenate([high, low], axis=1)


def scores_of(q, k):
    return lax.dot_general(
        q, jnp.concatenate([k, k], axis=1), (((1,), (1,)), ((), ())), preferred_element_type=jnp.float32
    )


def with_ones(v):
    return jnp.concatenate([v, jnp.ones_like(v)], axis=1)


def put_stats(lane, stats, h, m, l):
    stats = jnp.where(lane == h, m, stats)
    return jnp.where(lane == HEADS + h, l, stats)


def own_kernel(q_ref, kv_ref, acc_ref, stat_ref):
    shape = (HEADS * BROWS, BROWS)
    row = lax.broadcasted_iota(jnp.int32, shape, 0) % BROWS
    causal = row >= lax.broadcasted_iota(jnp.int32, shape, 1)
    lane = lax.broadcasted_iota(jnp.int32, (BROWS, 128), 1)
    for b in range(q_ref.shape[0] // BROWS):
        rows = slice(b * BROWS, (b + 1) * BROWS)
        q = scaled(jnp.concatenate([q_ref[rows, h * HD : (h + 1) * HD] for h in range(HEADS)], axis=0))
        s = jnp.where(causal, scores_of(q, kv_ref[rows, 0:HD]), LOW)
        m = jnp.max(s, axis=1, keepdims=True)
        p = jnp.exp2(s - m)
        pv = jnp.dot(p.astype(jnp.bfloat16), with_ones(kv_ref[rows, HD:]), preferred_element_type=jnp.float32)
        stats = jnp.zeros((BROWS, 128), jnp.float32)
        for h in range(HEADS):
            part = slice(h * BROWS, (h + 1) * BROWS)
            acc_ref[rows, h * HD : (h + 1) * HD] = pv[part, :HD]
            stats = put_stats(lane, stats, h, m[part], pv[part, HD:])
        stat_ref[rows, :] = stats


def fold(q, units, carry):
    m, l, a = carry
    s = jnp.concatenate([scores_of(q, u[:, 0:HD]) for u in units], axis=1)
    fresh = jnp.maximum(m, jnp.max(s, axis=1, keepdims=True))
    shrink = jnp.exp2(m - fresh)
    p = jnp.exp2(s - fresh[:, :1]).astype(jnp.bfloat16)
    v = jnp.concatenate([u[:, HD:] for u in units], axis=0)
    pv = jnp.dot(p, with_ones(v), preferred_element_type=jnp.float32)
    return fresh, l * shrink + pv[:, HD:], a * shrink + pv[:, :HD]


def phase_kernel(step, first, last, *refs):
    refs = list(refs)
    meta_ref, q_ref, kv0_ref, kv1_ref = refs[:4]
    del refs[:4]
    if not first:
        acc_in, ml_in = refs[:2]
        del refs[:2]
    if last:
        own_ref, own_stat_ref, far_ref, far_stat_ref, lst = refs
    else:
        acc_out, ml_out, lst = refs
    x_hi, core = meta_ref[4], meta_ref[5]
    lane16 = lax.broadcasted_iota(jnp.int32, (GROUP, 128), 1)

    def process(groups, base, at, want, n0, n1):
        size = groups * GROUP * HEADS
        starts = [pl.multiple_of(lst[base + i] * GROUP, GROUP) for i in range(groups)]
        q = scaled(
            jnp.concatenate(
                [q_ref[pl.ds(r, GROUP), h * HD : (h + 1) * HD] for r in starts for h in range(HEADS)], axis=0
            )
        )
        here = pl.ds(pl.multiple_of(at * GROUP * HEADS, GROUP * HEADS), size)
        if first:
            carry = (
                jnp.full((size, HD), LOW, jnp.float32),
                jnp.zeros((size, HD), jnp.float32),
                jnp.zeros((size, HD), jnp.float32),
            )
        else:
            ml = ml_in[here, :]
            wide = (size, HD)
            carry = (jnp.broadcast_to(ml[:, 0:1], wide), jnp.broadcast_to(ml[:, 1:2], wide), acc_in[here, :])
        places = []
        for i in range(n0):
            low = jnp.bitwise_and(i, (1 << core) - 1)
            places.append((kv0_ref, (((i - low) * 2) + (want << core)) + low))
        skip = want * 4 if (step == 4 and n1 == 4) else 0
        for i in range(n1):
            places.append((kv1_ref, skip + i))
        for i in range(0, len(places), 2):
            units = [
                ref[pl.ds(pl.multiple_of(e * UNIT, UNIT), UNIT), :] for ref, e in places[i : i + 2]
            ]
            carry = fold(q, units, carry)
        m, l, a = carry
        if not last:
            acc_out[here, :] = a
            lane = lax.broadcasted_iota(jnp.int32, (size, HD), 1)
            ml_out[here, :] = jnp.where(lane == 0, m, l)
            return
        for i, r in enumerate(starts):
            stats = jnp.zeros((GROUP, 128), jnp.float32)
            for h in range(HEADS):
                part = slice((i * HEADS + h) * GROUP, (i * HEADS + h + 1) * GROUP)
                stats = put_stats(lane16, stats, h, m[part], l[part])

            def store(ref, stat_ref, r, i=i, stats=stats):
                for h in range(HEADS):
                    part = slice((i * HEADS + h) * GROUP, (i * HEADS + h + 1) * GROUP)
                    ref[pl.ds(r, GROUP), h * HD : (h + 1) * HD] = a[part].astype(ref.dtype)
                stat_ref[pl.ds(r, GROUP), :] = stats

            @pl.when(r < 2 * BROWS)
            def _(r=r, store=store):
                store(own_ref, own_stat_ref, r)

            @pl.when(r >= 2 * BROWS)
            def _(r=r, store=store):
                store(far_ref, far_stat_ref, pl.multiple_of(r - 2 * BROWS, GROUP))

    offset = jnp.int32(0)
    for want in range(2):
        count = jnp.int32(0)
        for b in range(4):
            code = meta_ref[b]
            live = ((code & 255) + (GROUP - 1)) // GROUP
            live = jnp.where((code >> 8) == (x_hi ^ want), live, 0)

            def add(i, c, b=b, count=count):
                lst[want * LIST + count + i] = b * 8 + i
                return c

            lax.fori_loop(0, live, add, 0)
            count = count + live
        for i in range(3):
            lst[want * LIST + count + i] = jnp.where(count > 0, lst[want * LIST], 0)
        rest = count % 4
        fours = count // 4 + jnp.where(rest == 3, 1, 0)
        twos = jnp.where((rest == 1) | (rest == 2), 1, 0)
        if step == 2:
            variants = [(2, 4) if want == 0 else (2, 0)]
        elif step == 3:
            variants = [(2, 0), (2, 4)]
            picks = [core == want, core != want]
        else:
            variants = [(4, 4), (4, 8) if want else (4, 0)]
            picks = [core == 0, core == 1]
        for j, (n0, n1) in enumerate(variants):
            on = 1 if len(variants) == 1 else jnp.where(picks[j], 1, 0)

            def four(t, c, n0=n0, n1=n1, want=want, offset=offset):
                process(4, want * LIST + t * 4, offset + t * 4, want, n0, n1)
                return c

            def two(t, c, n0=n0, n1=n1, want=want, offset=offset, fours=fours):
                process(2, want * LIST + fours * 4, offset + fours * 4, want, n0, n1)
                return c

            lax.fori_loop(0, fours * on, four, 0)
            lax.fori_loop(0, twos * on, two, 0)
        offset = offset + fours * 4 + twos * 2


def phase(step, meta, q_all, kv0, kv1, state=None):
    first, last = step == 2, step == 4
    f32, b16 = jnp.float32, jnp.bfloat16
    if last:
        shapes = [((256, 1024), f32), ((256, 128), f32), ((256, 1024), b16), ((256, 128), f32)]
    else:
        shapes = [((STATE_ROWS, HD), f32)] * 2
    operands = [meta, q_all, kv0, kv1] + ([] if first else list(state))
    positions = kv0.shape[0]
    return pl.pallas_call(
        functools.partial(phase_kernel, step, first, last),
        out_shape=[jax.ShapeDtypeStruct(s, d) for s, d in shapes],
        in_specs=[SMEM] + [VMEM] * (len(operands) - 1),
        out_specs=[VMEM] * len(shapes),
        scratch_shapes=[pltpu.SMEM((2 * LIST,), jnp.int32)],
        input_output_aliases={4: 0, 5: 1} if step == 3 else {},
        compiler_params=pltpu.CompilerParams(vmem_limit_bytes=40 * 2**20),
        cost_estimate=pl.CostEstimate(
            flops=2 * 2560 * positions * 512, bytes_accessed=4 * 2**20, transcendentals=2560 * positions
        ),
        name=f"fold{step}",
    )(*operands)


def own_part(q, kv):
    return pl.pallas_call(
        own_kernel,
        out_shape=[
            jax.ShapeDtypeStruct((256, 1024), jnp.float32),
            jax.ShapeDtypeStruct((256, 128), jnp.float32),
        ],
        in_specs=[VMEM] * 2,
        out_specs=[VMEM] * 2,
        compiler_params=pltpu.CompilerParams(vmem_limit_bytes=32 * 2**20),
        cost_estimate=pl.CostEstimate(flops=2 * 2048 * 128 * 512, bytes_accessed=3 * 2**20, transcendentals=2048 * 128),
        name="own",
    )(q, kv)


def join_kernel(meta_ref, *refs):
    out_ref = refs[-1]
    parts = [(refs[i], refs[i + 1]) for i in range(0, 6, 2)]
    tall = 32
    for b in range(2):
        length = meta_ref[b] & 255
        for r in range(0, BROWS, tall):

            @pl.when(r < length)
            def _(b=b, r=r, length=length):
                rows = slice(b * BROWS + r, b * BROWS + r + tall)
                live = r + lax.broadcasted_iota(jnp.int32, (tall, HD), 0) < length
                stats = [s[rows, :] for _, s in parts]
                for h in range(HEADS):
                    cols = slice(h * HD, (h + 1) * HD)
                    m = [s[:, h : h + 1] for s in stats]
                    peak = functools.reduce(jnp.maximum, m)
                    w = [jnp.exp2(v - peak) for v in m]
                    total = sum(wi * s[:, HEADS + h : HEADS + h + 1] for wi, s in zip(w, stats))
                    blended = sum(wi / total * a[rows, cols].astype(jnp.float32) for wi, (a, _) in zip(w, parts))
                    out_ref[rows, cols] = jnp.where(live, blended, 0.0).astype(jnp.bfloat16)

            @pl.when(r >= length)
            def _(b=b, r=r):
                rows = slice(b * BROWS + r, b * BROWS + r + tall)
                out_ref[rows, :] = jnp.zeros((tall, 1024), jnp.bfloat16)


def join(meta, *parts):
    return pl.pallas_call(
        join_kernel,
        out_shape=jax.ShapeDtypeStruct((256, 1024), jnp.bfloat16),
        in_specs=[SMEM] + [VMEM] * 6,
        out_specs=VMEM,
        compiler_params=pltpu.CompilerParams(vmem_limit_bytes=32 * 2**20),
        name="join",
    )(meta, *parts)


def per_device(queries, answer_kv, prompt_kv, block_prompt, answer_len):
    piece = prompt_kv[0, :, 0, :]
    own_kv = answer_kv[:, 0, :]
    code = block_prompt[:, 0] * 256 + answer_len
    code_far = lax.ppermute(code, AXES, core_swap())
    q_far = lax.ppermute(queries, AXES, core_swap())
    place = jnp.stack([lax.axis_index("grp"), lax.axis_index("ctx") % 2]).astype(jnp.int32)
    meta = jnp.concatenate([code, code_far, place])
    held = [piece[:UNIT], piece[UNIT:]]
    came = None
    for step in range(4):
        came = [lax.ppermute(held[c], AXES, chip_swap(c, step)) for c in range(2)]
        if step == 0:
            own_acc, own_stat = own_part(queries, own_kv)
            q_all = jnp.concatenate([queries, q_far], axis=0)
        if step == 2:
            state = phase(2, meta, q_all, *held)
        if step == 3:
            state = phase(3, meta, q_all, *third, state)
        if step < 3:
            held = [jnp.concatenate([h, c], axis=0) for h, c in zip(held, came)]
        third = came
    near, near_stat, far, far_stat = phase(4, meta, q_all, *came, state)
    far = lax.ppermute(far, AXES, core_swap())
    far_stat = lax.ppermute(far_stat, AXES, core_swap())
    return join(meta, own_acc, own_stat, near, near_stat, far, far_stat)


def solution(mesh):
    placed = (
        P(("ctx", "grp"), "head"),
        P(("ctx", "grp"), "head", None),
        P("grp", "ctx", "head", None),
        P(("ctx", "grp"), None),
        P(("ctx", "grp")),
    )
    return jax.shard_map(
        per_device, mesh=mesh, in_specs=placed, out_specs=P(("ctx", "grp"), "head"), check_vma=False
    )
```

```python
import functools

import jax
import jax.numpy as jnp
import numpy as np
from jax import lax
from jax.experimental import pallas as pl
from jax.experimental.pallas import tpu as pltpu
from jax.sharding import PartitionSpec as P

HD = 128
BROWS = 128
HEADS = 8
BLOCK = 1024
CHUNK = 512
GROUP = 16
LIST = 48
STATE_ROWS = 40 * GROUP * HEADS
SCALE = float(np.log2(np.e) / np.sqrt(HD))
LOW = -1e30
VMEM = pl.BlockSpec(memory_space=pltpu.VMEM)
SMEM = pl.BlockSpec(memory_space=pltpu.SMEM)
AXES = ("ctx", "grp")

TURNS = {"even": lambda i: i ^ 1, "odd": lambda i: 3 - i, "across": lambda i: i ^ 2}


def index_of(x, y, core):
    return ((y * 2 + x % 2) * 2 + core) * 2 + x // 2


def ring_swap(stage, turn):
    pairs = []
    for x in range(4):
        for y in range(4):
            for core in range(2):
                to = (TURNS[turn](x), y) if core == stage else (x, TURNS[turn](y))
                pairs.append((index_of(x, y, core), index_of(*to, core)))
    return pairs


def core_swap():
    return [(index_of(x, y, c), index_of(x, y, 1 - c)) for x in range(4) for y in range(4) for c in range(2)]


def scaled(q):
    wide = q.astype(jnp.float32) * SCALE
    high = wide.astype(jnp.bfloat16)
    low = (wide - high.astype(jnp.float32)).astype(jnp.bfloat16)
    return jnp.concatenate([high, low], axis=1)


def scores_of(q, k):
    return lax.dot_general(
        q, jnp.concatenate([k, k], axis=1), (((1,), (1,)), ((), ())), preferred_element_type=jnp.float32
    )


def with_ones(v):
    return jnp.concatenate([v, jnp.ones_like(v)], axis=1)


def put_stats(lane, stats, h, m, l):
    stats = jnp.where(lane == h, m, stats)
    return jnp.where(lane == HEADS + h, l, stats)


def own_kernel(q_ref, kv_ref, acc_ref, stat_ref):
    shape = (HEADS * BROWS, BROWS)
    row = lax.broadcasted_iota(jnp.int32, shape, 0) % BROWS
    causal = row >= lax.broadcasted_iota(jnp.int32, shape, 1)
    lane = lax.broadcasted_iota(jnp.int32, (BROWS, 128), 1)
    for b in range(q_ref.shape[0] // BROWS):
        rows = slice(b * BROWS, (b + 1) * BROWS)
        q = scaled(jnp.concatenate([q_ref[rows, h * HD : (h + 1) * HD] for h in range(HEADS)], axis=0))
        s = jnp.where(causal, scores_of(q, kv_ref[rows, 0:HD]), LOW)
        m = jnp.max(s, axis=1, keepdims=True)
        p = jnp.exp2(s - m)
        pv = jnp.dot(p.astype(jnp.bfloat16), with_ones(kv_ref[rows, HD:]), preferred_element_type=jnp.float32)
        stats = jnp.zeros((BROWS, 128), jnp.float32)
        for h in range(HEADS):
            part = slice(h * BROWS, (h + 1) * BROWS)
            acc_ref[rows, h * HD : (h + 1) * HD] = pv[part, :HD]
            stats = put_stats(lane, stats, h, m[part], pv[part, HD:])
        stat_ref[rows, :] = stats


def fold(q, kv, carry):
    m, l, a = carry
    s = scores_of(q, kv[:, 0:HD])
    fresh = jnp.maximum(m, jnp.max(s, axis=1, keepdims=True))
    shrink = jnp.exp2(m - fresh)
    p = jnp.exp2(s - fresh[:, :1]).astype(jnp.bfloat16)
    pv = jnp.dot(p, with_ones(kv[:, HD:]), preferred_element_type=jnp.float32)
    return fresh, l * shrink + pv[:, HD:], a * shrink + pv[:, :HD]


def fold_kernel(number, *refs):
    meta_ref, q_ref, kv_ref = refs[:3]
    lst, sizes = refs[-2:]
    if number == 0:
        state_in = state = refs[3:6]
    elif number == 1:
        state_in, state = refs[3:6], refs[6:9]
    else:
        state_in = refs[3:6]
        own_ref, own_stat_ref, far_ref, far_stat_ref = refs[6:10]
        state = refs[10:13]
    x_hi, core = meta_ref[4], meta_ref[5]

    offset = jnp.int32(0)
    for want in range(2):
        count = jnp.int32(0)
        for b in range(4):
            code = meta_ref[b]
            live = ((code & 255) + (GROUP - 1)) // GROUP
            live = jnp.where((code >> 8) == (x_hi ^ want), live, 0)

            def add(i, c, b=b, count=count):
                lst[want * LIST + count + i] = b * 8 + i
                return c

            lax.fori_loop(0, live, add, 0)
            count = count + live
        for i in range(3):
            lst[want * LIST + count + i] = jnp.where(count > 0, lst[want * LIST], 0)
        rest = count % 4
        fours = count // 4 + jnp.where(rest == 3, 1, 0)
        twos = jnp.where((rest == 1) | (rest == 2), 1, 0)
        sizes[want * 3] = fours
        sizes[want * 3 + 1] = twos
        sizes[want * 3 + 2] = offset
        offset = offset + fours * 4 + twos * 2

    def over_tiles(want, step):
        fours, twos, at = sizes[want * 3], sizes[want * 3 + 1], sizes[want * 3 + 2]

        def four(t, c):
            step(4, want * LIST + t * 4, at + t * 4)
            return c

        def two(t, c):
            step(2, want * LIST + fours * 4, at + fours * 4)
            return c

        lax.fori_loop(0, fours, four, 0)
        lax.fori_loop(0, twos, two, 0)

    def rows_of(groups, base):
        return [pl.multiple_of(lst[base + i] * GROUP, GROUP) for i in range(groups)]

    def state_rows(groups, at):
        return pl.ds(pl.multiple_of(at * GROUP * HEADS, GROUP * HEADS), groups * GROUP * HEADS)

    def attend(blocks, source, groups, base, at):
        q = scaled(
            jnp.concatenate(
                [q_ref[pl.ds(r, GROUP), h * HD : (h + 1) * HD] for r in rows_of(groups, base) for h in range(HEADS)],
                axis=0,
            )
        )
        here = state_rows(groups, at)
        carry = tuple(ref[here, :] for ref in source)
        for block in blocks:
            for i in range(BLOCK // CHUNK):
                start = pl.multiple_of(block * BLOCK + i * CHUNK, CHUNK)
                carry = fold(q, kv_ref[pl.ds(start, CHUNK), :], carry)
        for ref, value in zip(state, carry):
            ref[here, :] = value

    if number == 0:

        def clear(groups, base, at):
            here = state_rows(groups, at)
            state[0][here, :] = jnp.full((groups * GROUP * HEADS, HD), LOW, jnp.float32)
            for ref in state[1:]:
                ref[here, :] = jnp.zeros((groups * GROUP * HEADS, HD), jnp.float32)

        def both(want, c):
            over_tiles(want, clear)
            return c

        lax.fori_loop(0, 2, both, 0)
    if number == 1:
        def both(want, c):
            first = jnp.where(want == 0, 0, 3)
            second = jnp.where((want ^ core) == 0, 1, 2)
            over_tiles(want, functools.partial(attend, (first, second), state_in))
            return c

        lax.fori_loop(0, 2, both, 0)
    else:
        if number == 2:

            def carry_over(groups, base, at):
                here = state_rows(groups, at)
                for ref, old in zip(state, state_in):
                    ref[here, :] = old[here, :]

        def each(block, c):
            want = jnp.where(core == 0, block, 0 if number == 0 else 1)
            over_tiles(want, functools.partial(attend, (block,), state))
            return c

        if number == 2:

            def both(want, c):
                over_tiles(want, carry_over)
                return c

            lax.fori_loop(0, 2, both, 0)
        lax.fori_loop(0, 2, each, 0)
    if number == 2:
        lane = lax.broadcasted_iota(jnp.int32, (GROUP, 128), 1)

        def emit(groups, base, at):
            for i, r in enumerate(rows_of(groups, base)):
                first = at * GROUP * HEADS + i * GROUP * HEADS

                def piece(ref, h, first=first):
                    return ref[pl.ds(pl.multiple_of(first + h * GROUP, GROUP), GROUP), :]

                stats = jnp.zeros((GROUP, 128), jnp.float32)
                for h in range(HEADS):
                    stats = put_stats(lane, stats, h, piece(state[0], h), piece(state[1], h))

                @pl.when(r < 2 * BROWS)
                def _(r=r, piece=piece, stats=stats):
                    for h in range(HEADS):
                        own_ref[pl.ds(r, GROUP), h * HD : (h + 1) * HD] = piece(state[2], h)
                    own_stat_ref[pl.ds(r, GROUP), :] = stats

                @pl.when(r >= 2 * BROWS)
                def _(r=r, piece=piece, stats=stats):
                    to = pl.ds(pl.multiple_of(r - 2 * BROWS, GROUP), GROUP)
                    for h in range(HEADS):
                        far_ref[to, h * HD : (h + 1) * HD] = piece(state[2], h).astype(jnp.bfloat16)
                    far_stat_ref[to, :] = stats

        def both_out(want, c):
            over_tiles(want, emit)
            return c

        lax.fori_loop(0, 2, both_out, 0)


def fold_call(number, meta, q_all, kv, state=()):
    f32, b16 = jnp.float32, jnp.bfloat16
    scratch = [pltpu.SMEM((2 * LIST,), jnp.int32), pltpu.SMEM((8,), jnp.int32)]
    if number == 2:
        shapes = [((256, 1024), f32), ((256, 128), f32), ((256, 1024), b16), ((256, 128), f32)]
        scratch = [pltpu.VMEM((STATE_ROWS, HD), f32)] * 3 + scratch
    else:
        shapes = [((STATE_ROWS, HD), f32)] * 3
    operands = [meta, q_all, kv, *state]
    return pl.pallas_call(
        functools.partial(fold_kernel, number),
        out_shape=[jax.ShapeDtypeStruct(s, d) for s, d in shapes],
        in_specs=[SMEM] + [VMEM] * (len(operands) - 1),
        out_specs=[VMEM] * len(shapes),
        scratch_shapes=scratch,
        input_output_aliases={3: 0, 4: 1, 5: 2} if number == 1 else {},
        compiler_params=pltpu.CompilerParams(vmem_limit_bytes=40 * 2**20),
        cost_estimate=pl.CostEstimate(
            flops=2 * 2560 * kv.shape[0] * 256, bytes_accessed=4 * 2**20, transcendentals=1280 * kv.shape[0]
        ),
        name=f"fold{number}",
    )(*operands)


def own_part(q, kv):
    return pl.pallas_call(
        own_kernel,
        out_shape=[
            jax.ShapeDtypeStruct((256, 1024), jnp.float32),
            jax.ShapeDtypeStruct((256, 128), jnp.float32),
        ],
        in_specs=[VMEM] * 2,
        out_specs=[VMEM] * 2,
        compiler_params=pltpu.CompilerParams(vmem_limit_bytes=32 * 2**20),
        cost_estimate=pl.CostEstimate(flops=2 * 2048 * 128 * 512, bytes_accessed=3 * 2**20, transcendentals=2048 * 128),
        name="own",
    )(q, kv)


def join_kernel(meta_ref, *refs):
    out_ref = refs[-1]
    parts = [(refs[i], refs[i + 1]) for i in range(0, 6, 2)]
    tall = 32
    for b in range(2):
        length = meta_ref[b] & 255
        for r in range(0, BROWS, tall):

            @pl.when(r < length)
            def _(b=b, r=r, length=length):
                rows = slice(b * BROWS + r, b * BROWS + r + tall)
                live = r + lax.broadcasted_iota(jnp.int32, (tall, HD), 0) < length
                stats = [s[rows, :] for _, s in parts]
                peak = functools.reduce(jnp.maximum, stats)
                w = [jnp.exp2(s - peak) for s in stats]
                total = sum(wi * pltpu.roll(s, 128 - HEADS, 1) for wi, s in zip(w, stats))
                w = [wi / total for wi in w]
                for h in range(HEADS):
                    cols = slice(h * HD, (h + 1) * HD)
                    blended = sum(wi[:, h : h + 1] * a[rows, cols].astype(jnp.float32) for wi, (a, _) in zip(w, parts))
                    out_ref[rows, cols] = jnp.where(live, blended, 0.0).astype(jnp.bfloat16)

            @pl.when(r >= length)
            def _(b=b, r=r):
                rows = slice(b * BROWS + r, b * BROWS + r + tall)
                out_ref[rows, :] = jnp.zeros((tall, 1024), jnp.bfloat16)


def join(meta, *parts):
    return pl.pallas_call(
        join_kernel,
        out_shape=jax.ShapeDtypeStruct((256, 1024), jnp.bfloat16),
        in_specs=[SMEM] + [VMEM] * 6,
        out_specs=VMEM,
        compiler_params=pltpu.CompilerParams(vmem_limit_bytes=32 * 2**20),
        name="join",
    )(meta, *parts)


def per_device(queries, answer_kv, prompt_kv, block_prompt, answer_len):
    piece = prompt_kv[0, :, 0, :]
    own_kv = answer_kv[:, 0, :]
    code = block_prompt[:, 0] * 256 + answer_len
    place = jnp.stack([lax.axis_index("grp"), lax.axis_index("ctx") & 1]).astype(jnp.int32)

    even, odd, across = [lax.ppermute(piece, AXES, ring_swap(0, turn)) for turn in ("even", "odd", "across")]
    code_far = lax.ppermute(code, AXES, core_swap())
    q_far = lax.ppermute(queries, AXES, core_swap())
    own_acc, own_stat = own_part(queries, own_kv)
    even, odd, across, code_far, q_far, own_acc, own_stat = lax.optimization_barrier(
        (even, odd, across, code_far, q_far, own_acc, own_stat)
    )
    held = [jnp.concatenate([piece, even], axis=0), jnp.concatenate([odd, across], axis=0)]
    by_even = [lax.ppermute(h, AXES, ring_swap(1, "even")) for h in held]
    by_odd = [lax.ppermute(h, AXES, ring_swap(1, "odd")) for h in held]
    meta = jnp.concatenate([code, code_far, place])
    q_all = jnp.concatenate([queries, q_far], axis=0)
    state = fold_call(0, meta, q_all, jnp.concatenate(held, axis=0))
    even0, odd1, state = lax.optimization_barrier((by_even[0], by_odd[1], state))
    last = [
        lax.ppermute(even0, AXES, ring_swap(1, "odd")),
        lax.ppermute(odd1, AXES, ring_swap(1, "even")),
    ]
    second = jnp.concatenate([even0, by_odd[0], by_even[1], odd1], axis=0)
    state = fold_call(1, meta, q_all, second, state)
    near, near_stat, far, far_stat = fold_call(2, meta, q_all, jnp.concatenate(last, axis=0), state)
    far = lax.ppermute(far, AXES, core_swap())
    far_stat = lax.ppermute(far_stat, AXES, core_swap())
    return join(meta, own_acc, own_stat, near, near_stat, far, far_stat)


def solution(mesh):
    placed = (
        P(("ctx", "grp"), "head"),
        P(("ctx", "grp"), "head", None),
        P("grp", "ctx", "head", None),
        P(("ctx", "grp"), None),
        P(("ctx", "grp")),
    )
    return jax.shard_map(
        per_device, mesh=mesh, in_specs=placed, out_specs=P(("ctx", "grp"), "head"), check_vma=False
    )
```

```python
import functools

import jax
import jax.numpy as jnp
import numpy as np
from jax import lax
from jax.experimental import pallas as pl
from jax.experimental.pallas import tpu as pltpu
from jax.sharding import PartitionSpec as P

HD = 128
BROWS = 128
HEADS = 8
BLOCK = 1024
GROUP = 16
TILE = 4
PLAN, INV, SIZES, META = 128, 40, 72, 80
STATE_ROWS = 9 * TILE * GROUP * HEADS
SCALE = float(np.log2(np.e) / np.sqrt(HD))
LOW = -1e30
VMEM = pl.BlockSpec(memory_space=pltpu.VMEM)
SMEM = pl.BlockSpec(memory_space=pltpu.SMEM)
AXES = ("ctx", "grp")

TURNS = {"even": lambda i: i ^ 1, "odd": lambda i: 3 - i, "across": lambda i: i ^ 2}


def index_of(x, y, core):
    return ((y * 2 + x % 2) * 2 + core) * 2 + x // 2


def ring_swap(stage, turn):
    pairs = []
    for x in range(4):
        for y in range(4):
            for core in range(2):
                to = (TURNS[turn](x), y) if core == stage else (x, TURNS[turn](y))
                pairs.append((index_of(x, y, core), index_of(*to, core)))
    return pairs


def core_swap():
    return [(index_of(x, y, c), index_of(x, y, 1 - c)) for x in range(4) for y in range(4) for c in range(2)]


def scaled(q):
    wide = q.astype(jnp.float32) * SCALE
    high = wide.astype(jnp.bfloat16)
    low = (wide - high.astype(jnp.float32)).astype(jnp.bfloat16)
    return jnp.concatenate([high, low], axis=1)


def scores_of(q, k):
    return lax.dot_general(
        q, jnp.concatenate([k, k], axis=1), (((1,), (1,)), ((), ())), preferred_element_type=jnp.float32
    )


def with_ones(v):
    return jnp.concatenate([v, jnp.ones_like(v)], axis=1)


def put_stats(lane, stats, h, m, l):
    stats = jnp.where(lane == h, m, stats)
    return jnp.where(lane == HEADS + h, l, stats)


def make_plan(meta_ref, plan_ref):
    for i in range(32):
        plan_ref[INV + i] = 0
    for i in range(6):
        plan_ref[META + i] = meta_ref[i]
    offset = jnp.int32(0)
    for want in range(2):
        count = jnp.int32(0)
        for b in range(4):
            code = meta_ref[b]
            live = ((code & 255) + (GROUP - 1)) // GROUP
            live = jnp.where((code >> 8) == (meta_ref[4] ^ want), live, 0)

            def add(i, c, b=b, at=offset + count):
                plan_ref[at + i] = b * 8 + i
                plan_ref[INV + b * 8 + i] = at + i
                return c

            lax.fori_loop(0, live, add, 0)
            count = count + live
        tiles = (count + (TILE - 1)) // TILE
        plan_ref[SIZES + want * 3] = count
        plan_ref[SIZES + want * 3 + 1] = tiles
        plan_ref[SIZES + want * 3 + 2] = offset
        offset = offset + tiles * TILE


def piece_of(place, h):
    return pl.ds(pl.multiple_of(place * (GROUP * HEADS) + h * GROUP, GROUP), GROUP)


def over_groups(plan_ref, step):
    for want in range(2):

        def one(i, c, want=want):
            step(plan_ref[SIZES + want * 3 + 2] + i)
            return c

        lax.fori_loop(0, plan_ref[SIZES + want * 3], one, 0)


def prep_kernel(meta_ref, q_ref, far_ref, kv_ref, plan_ref, qs_ref, m_ref, l_ref, a_ref):
    make_plan(meta_ref, plan_ref)

    def gather(place):
        group = plan_ref[place]

        def put(ref, r):
            for h in range(HEADS):
                qs_ref[piece_of(place, h), :] = scaled(ref[pl.ds(r, GROUP), h * HD : (h + 1) * HD])

        @pl.when(group < 16)
        def _():
            put(q_ref, pl.multiple_of(group * GROUP, GROUP))

        @pl.when(group >= 16)
        def _():
            put(far_ref, pl.multiple_of((group - 16) * GROUP, GROUP))
            here = pl.ds(pl.multiple_of(place * (GROUP * HEADS), GROUP * HEADS), GROUP * HEADS)
            m_ref[here, :] = jnp.full((GROUP * HEADS, HD), LOW, jnp.float32)
            l_ref[here, :] = jnp.zeros((GROUP * HEADS, HD), jnp.float32)
            a_ref[here, :] = jnp.zeros((GROUP * HEADS, HD), jnp.float32)

    over_groups(plan_ref, gather)
    shape = (HEADS * BROWS, BROWS)
    row = lax.broadcasted_iota(jnp.int32, shape, 0) % BROWS
    causal = row >= lax.broadcasted_iota(jnp.int32, shape, 1)
    for b in range(2):
        rows = slice(b * BROWS, (b + 1) * BROWS)
        q = scaled(jnp.concatenate([q_ref[rows, h * HD : (h + 1) * HD] for h in range(HEADS)], axis=0))
        s = jnp.where(causal, scores_of(q, kv_ref[rows, 0:HD]), LOW)
        m = jnp.max(s, axis=1, keepdims=True)
        p = jnp.exp2(s - m)
        pv = jnp.dot(p.astype(jnp.bfloat16), with_ones(kv_ref[rows, HD:]), preferred_element_type=jnp.float32)
        m = jnp.broadcast_to(m, (HEADS * BROWS, HD))
        for g in range(BROWS // GROUP):

            @pl.when(g * GROUP < (meta_ref[b] & 255))
            def _(b=b, g=g, m=m, pv=pv):
                for h in range(HEADS):
                    here = piece_of(plan_ref[INV + b * 8 + g], h)
                    part = slice(h * BROWS + g * GROUP, h * BROWS + (g + 1) * GROUP)
                    m_ref[here, :] = m[part]
                    l_ref[here, :] = pv[part, HD:]
                    a_ref[here, :] = pv[part, :HD]


def prep(meta, q, far, kv):
    return pl.pallas_call(
        prep_kernel,
        out_shape=[
            jax.ShapeDtypeStruct((PLAN,), jnp.int32),
            jax.ShapeDtypeStruct((STATE_ROWS, 2 * HD), jnp.bfloat16),
        ]
        + [jax.ShapeDtypeStruct((STATE_ROWS, HD), jnp.float32)] * 3,
        in_specs=[SMEM] + [VMEM] * 3,
        out_specs=[SMEM] + [VMEM] * 4,
        compiler_params=pltpu.CompilerParams(vmem_limit_bytes=40 * 2**20),
        cost_estimate=pl.CostEstimate(flops=2 * 2048 * 128 * 512, bytes_accessed=3 * 2**20, transcendentals=2048 * 128),
        name="prep",
    )(meta, q, far, kv)


def fold_kernel(number, *refs):
    refs = list(refs)
    plan_ref, qs_ref, kv_ref = refs[:3]
    m_in, l_in, a_in, m_ref, l_ref, a_ref = refs[3:9]
    item_at, item_kv, s0_ref, s1_ref = refs[-4:]
    core = plan_ref[META + 5]

    items = jnp.int32(0)
    for want in range(2):
        tiles, first = plan_ref[SIZES + want * 3 + 1], plan_ref[SIZES + want * 3 + 2]
        if number == 1:
            blocks = (0 if want == 0 else 3, jnp.where((want ^ core) == 0, 1, 2))
            many = 2
        else:
            blocks = (jnp.where(core == 0, want, 0), 1)
            many = jnp.where(core == 0, 1, 2 if (want == 0) == (number == 0) else 0)

        def add(t, c, first=first, blocks=blocks, many=many, items=items):
            for i in range(2):

                @pl.when(i < many)
                def _(i=i):
                    item_at[items + t * many + i] = first + t * TILE
                    item_kv[items + t * many + i] = blocks[i]

            return c

        lax.fori_loop(0, tiles, add, 0)
        items = items + tiles * many
    for i in range(2):
        item_at[items + i] = 0
        item_kv[items + i] = 0

    def rows(i):
        return pl.ds(pl.multiple_of(item_at[i] * (GROUP * HEADS), GROUP * HEADS), TILE * GROUP * HEADS)

    def positions(i):
        return pl.ds(pl.multiple_of(item_kv[i] * BLOCK, BLOCK), BLOCK)

    def score(i, s_ref):
        s_ref[...] = scores_of(qs_ref[rows(i), :], kv_ref[positions(i), 0:HD])

    def soften(i, s_ref):
        here = rows(i)
        s, m = s_ref[...], m_ref[here, :]
        fresh = jnp.maximum(m, jnp.max(s, axis=1, keepdims=True))
        shrink = jnp.exp2(m - fresh)
        p = jnp.exp2(s - jnp.concatenate([fresh] * (BLOCK // HD), axis=1)).astype(jnp.bfloat16)
        pv = jnp.dot(p, with_ones(kv_ref[positions(i), HD:]), preferred_element_type=jnp.float32)
        m_ref[here, :] = fresh
        l_ref[here, :] = l_ref[here, :] * shrink + pv[:, HD:]
        a_ref[here, :] = a_ref[here, :] * shrink + pv[:, :HD]

    score(0, s0_ref)

    def pair(j, c):
        i = j * 2
        score(i + 1, s1_ref)
        soften(i, s0_ref)
        score(i + 2, s0_ref)
        soften(i + 1, s1_ref)
        return c

    lax.fori_loop(0, items // 2, pair, 0)

    @pl.when(items % 2 == 1)
    def _():
        soften(items - 1, s0_ref)

    if number == 2:
        far_ref, far_stat_ref = refs[9:11]
        lane = lax.broadcasted_iota(jnp.int32, (GROUP, 128), 1)

        def emit(place):
            group = plan_ref[place]

            @pl.when(group >= 16)
            def _():
                to = pl.ds(pl.multiple_of((group - 16) * GROUP, GROUP), GROUP)
                stats = jnp.zeros((GROUP, 128), jnp.float32)
                for h in range(HEADS):
                    here = piece_of(place, h)
                    stats = put_stats(lane, stats, h, m_ref[here, :], l_ref[here, :])
                    far_ref[to, h * HD : (h + 1) * HD] = a_ref[here, :].astype(jnp.bfloat16)
                far_stat_ref[to, :] = stats

        over_groups(plan_ref, emit)


def fold_call(number, plan, qs, kv, state):
    f32, b16 = jnp.float32, jnp.bfloat16
    shapes = [((STATE_ROWS, HD), f32)] * 3
    if number == 2:
        shapes += [((256, 1024), b16), ((256, 128), f32)]
    operands = [plan, qs, kv, *state]
    wide = (TILE * GROUP * HEADS, BLOCK)
    return pl.pallas_call(
        functools.partial(fold_kernel, number),
        out_shape=[jax.ShapeDtypeStruct(s, d) for s, d in shapes],
        in_specs=[SMEM] + [VMEM] * (len(operands) - 1),
        out_specs=[VMEM] * len(shapes),
        scratch_shapes=[pltpu.SMEM((48,), jnp.int32)] * 2 + [pltpu.VMEM(wide, f32)] * 2,
        input_output_aliases={3: 0, 4: 1, 5: 2},
        compiler_params=pltpu.CompilerParams(vmem_limit_bytes=40 * 2**20),
        cost_estimate=pl.CostEstimate(
            flops=2 * 2560 * kv.shape[0] * 256, bytes_accessed=4 * 2**20, transcendentals=1280 * kv.shape[0]
        ),
        name=f"fold{number}",
    )(*operands)


def join_kernel(plan_ref, m_ref, l_ref, a_ref, far_ref, far_stat_ref, out_ref):
    def four(i, c):
        b = i // 2
        first = (i - b * 2) * 4
        length = (plan_ref[META + b] & 255) - first * GROUP

        @pl.when(length > 0)
        def _():
            for g in range(4):
                group = i * 4 + g
                rows = pl.ds(pl.multiple_of(group * GROUP, GROUP), GROUP)
                place = plan_ref[INV + group]
                live = lax.broadcasted_iota(jnp.int32, (GROUP, HD), 0) < length - g * GROUP
                stats = far_stat_ref[rows, :]
                for h in range(HEADS):
                    cols = slice(h * HD, (h + 1) * HD)
                    here = piece_of(place, h)
                    m, far_m = m_ref[here, :], stats[:, h : h + 1]
                    peak = jnp.maximum(m, far_m)
                    w, far_w = jnp.exp2(m - peak), jnp.exp2(far_m - peak)
                    total = w * l_ref[here, :] + far_w * stats[:, HEADS + h : HEADS + h + 1]
                    blended = w * a_ref[here, :] + far_w * far_ref[rows, cols].astype(jnp.float32)
                    out_ref[rows, cols] = jnp.where(live, blended / total, 0.0).astype(jnp.bfloat16)

        @pl.when(length <= 0)
        def _():
            rows = pl.ds(pl.multiple_of(i * 4 * GROUP, 4 * GROUP), 4 * GROUP)
            out_ref[rows, :] = jnp.zeros((4 * GROUP, HEADS * HD), jnp.bfloat16)

        return c

    lax.fori_loop(0, 4, four, 0)


def join(plan, state, far, far_stat):
    return pl.pallas_call(
        join_kernel,
        out_shape=jax.ShapeDtypeStruct((256, 1024), jnp.bfloat16),
        in_specs=[SMEM] + [VMEM] * 5,
        out_specs=VMEM,
        compiler_params=pltpu.CompilerParams(vmem_limit_bytes=32 * 2**20),
        name="join",
    )(plan, *state, far, far_stat)


def per_device(queries, answer_kv, prompt_kv, block_prompt, answer_len):
    piece = prompt_kv[0, :, 0, :]
    own_kv = answer_kv[:, 0, :]
    code = block_prompt[:, 0] * 256 + answer_len
    place = jnp.stack([lax.axis_index("grp"), lax.axis_index("ctx") & 1]).astype(jnp.int32)

    even, odd, across = [lax.ppermute(piece, AXES, ring_swap(0, turn)) for turn in ("even", "odd", "across")]
    code_far = lax.ppermute(code, AXES, core_swap())
    q_far = lax.ppermute(queries, AXES, core_swap())
    meta = jnp.concatenate([code, code_far, place])
    plan, qs, *state = prep(meta, queries, q_far, own_kv)
    even, odd, across, qs, state = lax.optimization_barrier((even, odd, across, qs, state))
    held = [jnp.concatenate([piece, even], axis=0), jnp.concatenate([odd, across], axis=0)]
    by_even = [lax.ppermute(h, AXES, ring_swap(1, "even")) for h in held]
    by_odd = [lax.ppermute(h, AXES, ring_swap(1, "odd")) for h in held]
    state = fold_call(0, plan, qs, jnp.concatenate(held, axis=0), state)
    even0, odd1, state = lax.optimization_barrier((by_even[0], by_odd[1], state))
    last = [
        lax.ppermute(even0, AXES, ring_swap(1, "odd")),
        lax.ppermute(odd1, AXES, ring_swap(1, "even")),
    ]
    second = jnp.concatenate([even0, by_odd[0], by_even[1], odd1], axis=0)
    state = fold_call(1, plan, qs, second, state)
    *state, far, far_stat = fold_call(2, plan, qs, jnp.concatenate(last, axis=0), state)
    far = lax.ppermute(far, AXES, core_swap())
    far_stat = lax.ppermute(far_stat, AXES, core_swap())
    return join(plan, state, far, far_stat)


def solution(mesh):
    placed = (
        P(("ctx", "grp"), "head"),
        P(("ctx", "grp"), "head", None),
        P("grp", "ctx", "head", None),
        P(("ctx", "grp"), None),
        P(("ctx", "grp")),
    )
    return jax.shard_map(
        per_device, mesh=mesh, in_specs=placed, out_specs=P(("ctx", "grp"), "head"), check_vma=False
    )
```

```python
import functools

import jax
import jax.numpy as jnp
import numpy as np
from jax import lax
from jax.experimental import pallas as pl
from jax.experimental.pallas import tpu as pltpu
from jax.sharding import PartitionSpec as P

HD = 128
BROWS = 128
HEADS = 8
BLOCK = 1024
GROUP = 16
TILE = 4
PLAN, INV, SIZES, META = 128, 40, 72, 80
STATE_ROWS = 9 * TILE * GROUP * HEADS
SCALE = float(np.log2(np.e) / np.sqrt(HD))
LOW = -1e30
VMEM = pl.BlockSpec(memory_space=pltpu.VMEM)
SMEM = pl.BlockSpec(memory_space=pltpu.SMEM)
HBM = pl.BlockSpec(memory_space=pltpu.HBM)
AXES = ("ctx", "grp")

TURNS = {"even": lambda i: i ^ 1, "odd": lambda i: 3 - i, "across": lambda i: i ^ 2}


def index_of(x, y, core):
    return ((y * 2 + x % 2) * 2 + core) * 2 + x // 2


def ring_swap(stage, turn):
    pairs = []
    for x in range(4):
        for y in range(4):
            for core in range(2):
                to = (TURNS[turn](x), y) if core == stage else (x, TURNS[turn](y))
                pairs.append((index_of(x, y, core), index_of(*to, core)))
    return pairs


def core_swap():
    return [(index_of(x, y, c), index_of(x, y, 1 - c)) for x in range(4) for y in range(4) for c in range(2)]


def scaled(q):
    wide = q.astype(jnp.float32) * SCALE
    high = wide.astype(jnp.bfloat16)
    low = (wide - high.astype(jnp.float32)).astype(jnp.bfloat16)
    return jnp.concatenate([high, low], axis=1)


def scores_of(q, k):
    return lax.dot_general(
        q, jnp.concatenate([k, k], axis=1), (((1,), (1,)), ((), ())), preferred_element_type=jnp.float32
    )


def with_ones(v):
    return jnp.concatenate([v, jnp.ones_like(v)], axis=1)


def put_stats(lane, stats, h, m, l):
    stats = jnp.where(lane == h, m, stats)
    return jnp.where(lane == HEADS + h, l, stats)


def make_plan(meta_ref, plan_ref):
    for i in range(32):
        plan_ref[INV + i] = 0
    for i in range(4):
        plan_ref[META + i] = meta_ref[4 + i]
    plan_ref[META + 5] = meta_ref[9]
    offset = jnp.int32(0)
    for want in range(2):
        count = jnp.int32(0)
        for b in range(4):
            live = (meta_ref[4 + b] + (GROUP - 1)) // GROUP
            live = jnp.where(meta_ref[b] == (meta_ref[8] ^ want), live, 0)

            def add(i, c, b=b, at=offset + count):
                plan_ref[at + i] = b * 8 + i
                plan_ref[INV + b * 8 + i] = at + i
                return c

            lax.fori_loop(0, live, add, 0)
            count = count + live
        tiles = (count + (TILE - 1)) // TILE
        plan_ref[SIZES + want * 3] = count
        plan_ref[SIZES + want * 3 + 1] = tiles
        plan_ref[SIZES + want * 3 + 2] = offset
        offset = offset + tiles * TILE


def piece_of(place, h):
    return pl.ds(pl.multiple_of(place * (GROUP * HEADS) + h * GROUP, GROUP), GROUP)


def over_groups(plan_ref, step):
    for want in range(2):

        def one(i, c, want=want):
            step(plan_ref[SIZES + want * 3 + 2] + i)
            return c

        lax.fori_loop(0, plan_ref[SIZES + want * 3], one, 0)


def prep_kernel(
    meta_ref, q_hbm, far_ref, kv_hbm, piece_hbm, plan_ref, qs_ref, m_ref, l_ref, a_ref, piece_ref, q_ref, kv_ref, sems
):
    copies = [
        pltpu.make_async_copy(src, dst, sems.at[i])
        for i, (src, dst) in enumerate(((q_hbm, q_ref), (kv_hbm, kv_ref), (piece_hbm, piece_ref)))
    ]
    for copy in copies:
        copy.start()
    make_plan(meta_ref, plan_ref)
    for copy in copies:
        copy.wait()

    def gather(place):
        group = plan_ref[place]

        def put(ref, r):
            for h in range(HEADS):
                qs_ref[piece_of(place, h), :] = scaled(ref[pl.ds(r, GROUP), h * HD : (h + 1) * HD])

        @pl.when(group < 16)
        def _():
            put(q_ref, pl.multiple_of(group * GROUP, GROUP))

        @pl.when(group >= 16)
        def _():
            put(far_ref, pl.multiple_of((group - 16) * GROUP, GROUP))
            here = pl.ds(pl.multiple_of(place * (GROUP * HEADS), GROUP * HEADS), GROUP * HEADS)
            m_ref[here, :] = jnp.full((GROUP * HEADS, HD), LOW, jnp.float32)
            l_ref[here, :] = jnp.zeros((GROUP * HEADS, HD), jnp.float32)
            a_ref[here, :] = jnp.zeros((GROUP * HEADS, HD), jnp.float32)

    over_groups(plan_ref, gather)
    shape = (HEADS * BROWS, BROWS)
    row = lax.broadcasted_iota(jnp.int32, shape, 0) % BROWS
    causal = row >= lax.broadcasted_iota(jnp.int32, shape, 1)
    for b in range(2):
        rows = slice(b * BROWS, (b + 1) * BROWS)
        q = scaled(jnp.concatenate([q_ref[rows, h * HD : (h + 1) * HD] for h in range(HEADS)], axis=0))
        s = jnp.where(causal, scores_of(q, kv_ref[rows, 0:HD]), LOW)
        m = jnp.max(s, axis=1, keepdims=True)
        p = jnp.exp2(s - m)
        pv = jnp.dot(p.astype(jnp.bfloat16), with_ones(kv_ref[rows, HD:]), preferred_element_type=jnp.float32)
        m = jnp.broadcast_to(m, (HEADS * BROWS, HD))
        for g in range(BROWS // GROUP):

            @pl.when(g * GROUP < meta_ref[4 + b])
            def _(b=b, g=g, m=m, pv=pv):
                for h in range(HEADS):
                    here = piece_of(plan_ref[INV + b * 8 + g], h)
                    part = slice(h * BROWS + g * GROUP, h * BROWS + (g + 1) * GROUP)
                    m_ref[here, :] = m[part]
                    l_ref[here, :] = pv[part, HD:]
                    a_ref[here, :] = pv[part, :HD]


def prep(meta, q, far, kv, piece):
    return pl.pallas_call(
        prep_kernel,
        out_shape=[
            jax.ShapeDtypeStruct((PLAN,), jnp.int32),
            jax.ShapeDtypeStruct((STATE_ROWS, 2 * HD), jnp.bfloat16),
        ]
        + [jax.ShapeDtypeStruct((STATE_ROWS, HD), jnp.float32)] * 3
        + [jax.ShapeDtypeStruct(piece.shape, piece.dtype)],
        in_specs=[SMEM, HBM, VMEM, HBM, HBM],
        out_specs=[SMEM] + [VMEM] * 5,
        scratch_shapes=[
            pltpu.VMEM(q.shape, q.dtype),
            pltpu.VMEM(kv.shape, kv.dtype),
            pltpu.SemaphoreType.DMA((3,)),
        ],
        compiler_params=pltpu.CompilerParams(vmem_limit_bytes=40 * 2**20),
        cost_estimate=pl.CostEstimate(flops=2 * 2048 * 128 * 512, bytes_accessed=3 * 2**20, transcendentals=2048 * 128),
        name="prep",
    )(meta, q, far, kv, piece)


def fold_kernel(number, *refs):
    refs = list(refs)
    plan_ref, qs_ref, kv_ref = refs[:3]
    m_in, l_in, a_in, m_ref, l_ref, a_ref = refs[3:9]
    item_at, item_kv, s0_ref, s1_ref = refs[-4:]
    core = plan_ref[META + 5]

    items = jnp.int32(0)
    for want in range(2):
        tiles, first = plan_ref[SIZES + want * 3 + 1], plan_ref[SIZES + want * 3 + 2]
        if number == 1:
            blocks, many = (want, 0), 1
        elif number == 2:
            blocks, many = (want ^ core, 0), 1
        else:
            blocks = (jnp.where(core == 0, want, 0), 1)
            many = jnp.where(core == 0, 1, 2 if (want == 0) == (number == 0) else 0)

        def add(t, c, first=first, blocks=blocks, many=many, items=items):
            for i in range(1 if number in (1, 2) else 2):

                @pl.when(i < many)
                def _(i=i):
                    item_at[items + t * many + i] = first + t * TILE
                    item_kv[items + t * many + i] = blocks[i]

            return c

        lax.fori_loop(0, tiles, add, 0)
        items = items + tiles * many
    for i in range(2):
        item_at[items + i] = 0
        item_kv[items + i] = 0

    def rows(i):
        return pl.ds(pl.multiple_of(item_at[i] * (GROUP * HEADS), GROUP * HEADS), TILE * GROUP * HEADS)

    def positions(i):
        return pl.ds(pl.multiple_of(item_kv[i] * BLOCK, BLOCK), BLOCK)

    def score(i, s_ref):
        s_ref[...] = scores_of(qs_ref[rows(i), :], kv_ref[positions(i), 0:HD])

    def soften(i, s_ref):
        here = rows(i)
        s, m = s_ref[...], m_ref[here, :]
        fresh = jnp.maximum(m, jnp.max(s, axis=1, keepdims=True))
        shrink = jnp.exp2(m - fresh)
        p = jnp.exp2(s - jnp.concatenate([fresh] * (BLOCK // HD), axis=1)).astype(jnp.bfloat16)
        pv = jnp.dot(p, with_ones(kv_ref[positions(i), HD:]), preferred_element_type=jnp.float32)
        m_ref[here, :] = fresh
        l_ref[here, :] = l_ref[here, :] * shrink + pv[:, HD:]
        a_ref[here, :] = a_ref[here, :] * shrink + pv[:, :HD]

    score(0, s0_ref)

    def pair(j, c):
        i = j * 2
        score(i + 1, s1_ref)
        soften(i, s0_ref)
        score(i + 2, s0_ref)
        soften(i + 1, s1_ref)
        return c

    lax.fori_loop(0, items // 2, pair, 0)

    @pl.when(items % 2 == 1)
    def _():
        soften(items - 1, s0_ref)

    if number == 3:
        far_ref, far_stat_ref = refs[9:11]
        lane = lax.broadcasted_iota(jnp.int32, (GROUP, 128), 1)

        def emit(place):
            group = plan_ref[place]

            @pl.when(group >= 16)
            def _():
                to = pl.ds(pl.multiple_of((group - 16) * GROUP, GROUP), GROUP)
                stats = jnp.zeros((GROUP, 128), jnp.float32)
                for h in range(HEADS):
                    here = piece_of(place, h)
                    stats = put_stats(lane, stats, h, m_ref[here, :], l_ref[here, :])
                    far_ref[to, h * HD : (h + 1) * HD] = a_ref[here, :].astype(jnp.bfloat16)
                far_stat_ref[to, :] = stats

        over_groups(plan_ref, emit)


def fold_call(number, plan, qs, kv, state):
    f32, b16 = jnp.float32, jnp.bfloat16
    shapes = [((STATE_ROWS, HD), f32)] * 3
    if number == 3:
        shapes += [((256, 1024), b16), ((256, 128), f32)]
    operands = [plan, qs, kv, *state]
    wide = (TILE * GROUP * HEADS, BLOCK)
    return pl.pallas_call(
        functools.partial(fold_kernel, number),
        out_shape=[jax.ShapeDtypeStruct(s, d) for s, d in shapes],
        in_specs=[SMEM] + [VMEM] * (len(operands) - 1),
        out_specs=[VMEM] * len(shapes),
        scratch_shapes=[pltpu.SMEM((48,), jnp.int32)] * 2 + [pltpu.VMEM(wide, f32)] * 2,
        input_output_aliases={3: 0, 4: 1, 5: 2},
        compiler_params=pltpu.CompilerParams(vmem_limit_bytes=40 * 2**20),
        cost_estimate=pl.CostEstimate(
            flops=2 * 2560 * kv.shape[0] * 256, bytes_accessed=4 * 2**20, transcendentals=1280 * kv.shape[0]
        ),
        name=f"fold{number}",
    )(*operands)


def join_kernel(plan_ref, m_ref, l_ref, a_ref, far_ref, far_stat_ref, out_ref):
    def four(i, c):
        b = i // 2
        first = (i - b * 2) * 4
        length = plan_ref[META + b] - first * GROUP

        @pl.when(length > 0)
        def _():
            for g in range(4):
                group = i * 4 + g
                rows = pl.ds(pl.multiple_of(group * GROUP, GROUP), GROUP)
                place = plan_ref[INV + group]
                live = lax.broadcasted_iota(jnp.int32, (GROUP, HD), 0) < length - g * GROUP
                stats = far_stat_ref[rows, :]
                for h in range(HEADS):
                    cols = slice(h * HD, (h + 1) * HD)
                    here = piece_of(place, h)
                    m, far_m = m_ref[here, :], stats[:, h : h + 1]
                    peak = jnp.maximum(m, far_m)
                    w, far_w = jnp.exp2(m - peak), jnp.exp2(far_m - peak)
                    total = w * l_ref[here, :] + far_w * stats[:, HEADS + h : HEADS + h + 1]
                    blended = w * a_ref[here, :] + far_w * far_ref[rows, cols].astype(jnp.float32)
                    out_ref[rows, cols] = jnp.where(live, blended / total, 0.0).astype(jnp.bfloat16)

        @pl.when(length <= 0)
        def _():
            rows = pl.ds(pl.multiple_of(i * 4 * GROUP, 4 * GROUP), 4 * GROUP)
            out_ref[rows, :] = jnp.zeros((4 * GROUP, HEADS * HD), jnp.bfloat16)

        return c

    lax.fori_loop(0, 4, four, 0)


def join(plan, state, far, far_stat):
    return pl.pallas_call(
        join_kernel,
        out_shape=jax.ShapeDtypeStruct((256, 1024), jnp.bfloat16),
        in_specs=[SMEM] + [VMEM] * 5,
        out_specs=VMEM,
        compiler_params=pltpu.CompilerParams(vmem_limit_bytes=32 * 2**20),
        name="join",
    )(plan, *state, far, far_stat)


def per_device(queries, answer_kv, prompt_kv, block_prompt, answer_len):
    piece = prompt_kv[0, :, 0, :]
    own_kv = answer_kv[:, 0, :]
    targets = block_prompt[:, 0]
    place = jnp.stack([lax.axis_index("grp"), lax.axis_index("ctx") & 1]).astype(jnp.int32)

    even, odd, across = [lax.ppermute(piece, AXES, ring_swap(0, turn)) for turn in ("even", "odd", "across")]
    targets_far, len_far, q_far = [lax.ppermute(v, AXES, core_swap()) for v in (targets, answer_len, queries)]
    meta = jnp.concatenate([targets, targets_far, answer_len, len_far, place])
    plan, qs, *state, piece_near = prep(meta, queries, q_far, own_kv, piece)
    even, odd, across, piece_near = lax.optimization_barrier((even, odd, across, piece_near))
    held = [jnp.concatenate([piece_near, even], axis=0), jnp.concatenate([odd, across], axis=0)]
    even0, even1 = [lax.ppermute(h, AXES, ring_swap(1, "even")) for h in held]
    odd0, odd1 = [lax.ppermute(h, AXES, ring_swap(1, "odd")) for h in held]
    state = fold_call(0, plan, qs, jnp.concatenate(held, axis=0), state)
    even0, odd1, state = lax.optimization_barrier((even0, odd1, state))
    last = [
        lax.ppermute(even0, AXES, ring_swap(1, "odd")),
        lax.ppermute(odd1, AXES, ring_swap(1, "even")),
    ]
    state = fold_call(1, plan, qs, jnp.concatenate([even0, odd1], axis=0), state)
    odd0, even1, state = lax.optimization_barrier((odd0, even1, state))
    state = fold_call(2, plan, qs, jnp.concatenate([odd0, even1], axis=0), state)
    *state, far, far_stat = fold_call(3, plan, qs, jnp.concatenate(last, axis=0), state)
    far = lax.ppermute(far, AXES, core_swap())
    far_stat = lax.ppermute(far_stat, AXES, core_swap())
    return join(plan, state, far, far_stat)


def solution(mesh):
    placed = (
        P(("ctx", "grp"), "head"),
        P(("ctx", "grp"), "head", None),
        P("grp", "ctx", "head", None),
        P(("ctx", "grp"), None),
        P(("ctx", "grp")),
    )
    return jax.shard_map(
        per_device, mesh=mesh, in_specs=placed, out_specs=P(("ctx", "grp"), "head"), check_vma=False
    )
```

```python
import functools

import jax
import jax.numpy as jnp
import numpy as np
from jax import lax
from jax.experimental import pallas as pl
from jax.experimental.pallas import tpu as pltpu
from jax.sharding import PartitionSpec as P

HD = 128
BROWS = 128
HEADS = 8
BLOCK = 1024
GROUP = 16
TILE = 4
LIST = 8
SPARE = 32
STATE_ROWS = 33 * GROUP * HEADS
SCALE = float(np.log2(np.e) / np.sqrt(HD))
LOW = -1e30
VMEM = pl.BlockSpec(memory_space=pltpu.VMEM)
SMEM = pl.BlockSpec(memory_space=pltpu.SMEM)
AXES = ("ctx", "grp")

TURNS = {"even": lambda i: i ^ 1, "odd": lambda i: 3 - i, "across": lambda i: i ^ 2}


def index_of(x, y, core):
    return ((y * 2 + x % 2) * 2 + core) * 2 + x // 2


def ring_swap(stage, turn):
    pairs = []
    for x in range(4):
        for y in range(4):
            for core in range(2):
                to = (TURNS[turn](x), y) if core == stage else (x, TURNS[turn](y))
                pairs.append((index_of(x, y, core), index_of(*to, core)))
    return pairs


def core_swap():
    return [(index_of(x, y, c), index_of(x, y, 1 - c)) for x in range(4) for y in range(4) for c in range(2)]


def scaled(q):
    wide = q.astype(jnp.float32) * SCALE
    high = wide.astype(jnp.bfloat16)
    low = (wide - high.astype(jnp.float32)).astype(jnp.bfloat16)
    return jnp.concatenate([high, low], axis=1)


def scores_of(q, k):
    return lax.dot_general(
        q, jnp.concatenate([k, k], axis=1), (((1,), (1,)), ((), ())), preferred_element_type=jnp.float32
    )


def with_ones(v):
    return jnp.concatenate([v, jnp.ones_like(v)], axis=1)


def put_stats(lane, stats, h, m, l):
    stats = jnp.where(lane == h, m, stats)
    return jnp.where(lane == HEADS + h, l, stats)


def make_plan(meta_ref, plan_ref):
    offset = jnp.int32(0)
    for want in range(2):
        count = jnp.int32(0)
        for b in range(4):
            code = meta_ref[b]
            live = ((code & 255) + (GROUP - 1)) // GROUP
            live = jnp.where((code >> 8) == (meta_ref[4] ^ want), live, 0)

            def add(i, c, b=b, at=LIST + offset + count):
                plan_ref[at + i] = b * 8 + i
                return c

            lax.fori_loop(0, live, add, 0)
            count = count + live
        tiles = (count + (TILE - 1)) // TILE
        for i in range(TILE - 1):
            plan_ref[LIST + offset + count + i] = SPARE
        plan_ref[want] = tiles
        offset = offset + tiles * TILE
    plan_ref[2] = meta_ref[5]


def rows_of(group):
    return pl.ds(pl.multiple_of(group * (GROUP * HEADS), GROUP * HEADS), GROUP * HEADS)


def prep_kernel(meta_ref, q_ref, far_ref, kv_ref, plan_ref, qs_ref, m_ref, l_ref, a_ref):
    make_plan(meta_ref, plan_ref)
    shape = (HEADS * BROWS, BROWS)
    row = lax.broadcasted_iota(jnp.int32, shape, 0) % BROWS
    causal = row >= lax.broadcasted_iota(jnp.int32, shape, 1)
    for b in range(2):
        rows = slice(b * BROWS, (b + 1) * BROWS)
        q = scaled(jnp.concatenate([q_ref[rows, h * HD : (h + 1) * HD] for h in range(HEADS)], axis=0))
        s = jnp.where(causal, scores_of(q, kv_ref[rows, 0:HD]), LOW)
        m = jnp.max(s, axis=1, keepdims=True)
        p = jnp.exp2(s - m)
        pv = jnp.dot(p.astype(jnp.bfloat16), with_ones(kv_ref[rows, HD:]), preferred_element_type=jnp.float32)
        m = jnp.broadcast_to(m, (HEADS * BROWS, HD))
        for g in range(8):
            for h in range(HEADS):
                here = slice(((b * 8 + g) * HEADS + h) * GROUP, ((b * 8 + g) * HEADS + h + 1) * GROUP)
                part = slice(h * BROWS + g * GROUP, h * BROWS + (g + 1) * GROUP)
                qs_ref[here, :] = q[part]
                m_ref[here, :] = m[part]
                l_ref[here, :] = pv[part, HD:]
                a_ref[here, :] = pv[part, :HD]
    for g in range(16):
        for h in range(HEADS):
            here = slice(((16 + g) * HEADS + h) * GROUP, ((16 + g) * HEADS + h + 1) * GROUP)
            qs_ref[here, :] = scaled(far_ref[g * GROUP : (g + 1) * GROUP, h * HD : (h + 1) * HD])
    rest = slice(16 * GROUP * HEADS, STATE_ROWS)
    size = (STATE_ROWS - 16 * GROUP * HEADS, HD)
    m_ref[rest, :] = jnp.full(size, LOW, jnp.float32)
    l_ref[rest, :] = jnp.zeros(size, jnp.float32)
    a_ref[rest, :] = jnp.zeros(size, jnp.float32)
    qs_ref[SPARE * GROUP * HEADS : STATE_ROWS, :] = jnp.zeros((GROUP * HEADS, 2 * HD), jnp.bfloat16)


def prep(meta, q, far, kv):
    return pl.pallas_call(
        prep_kernel,
        out_shape=[
            jax.ShapeDtypeStruct((64,), jnp.int32),
            jax.ShapeDtypeStruct((STATE_ROWS, 2 * HD), jnp.bfloat16),
        ]
        + [jax.ShapeDtypeStruct((STATE_ROWS, HD), jnp.float32)] * 3,
        in_specs=[SMEM] + [VMEM] * 3,
        out_specs=[SMEM] + [VMEM] * 4,
        compiler_params=pltpu.CompilerParams(vmem_limit_bytes=40 * 2**20),
        cost_estimate=pl.CostEstimate(flops=2 * 2048 * 128 * 512, bytes_accessed=3 * 2**20, transcendentals=2048 * 128),
        name="prep",
    )(meta, q, far, kv)


def fold_kernel(number, *refs):
    refs = list(refs)
    plan_ref, qs_ref, kv_ref = refs[:3]
    m_ref, l_ref, a_ref = refs[6:9]
    item_at, item_kv, s0_ref, s1_ref = refs[-4:]
    core = plan_ref[2]

    items, first = jnp.int32(0), jnp.int32(LIST)
    for want in range(2):
        tiles = plan_ref[want]
        if number == 1:
            blocks, many = (want, 0), 1
        elif number == 2:
            blocks, many = (want ^ core, 0), 1
        else:
            blocks = (jnp.where(core == 0, want, 0), 1)
            many = jnp.where(core == 0, 1, 2 if (want == 0) == (number == 0) else 0)

        def add(t, c, first=first, blocks=blocks, many=many, items=items):
            for i in range(1 if number in (1, 2) else 2):

                @pl.when(i < many)
                def _(i=i):
                    item_at[items + t * many + i] = first + t * TILE
                    item_kv[items + t * many + i] = blocks[i]

            return c

        lax.fori_loop(0, tiles, add, 0)
        items = items + tiles * many
        first = first + tiles * TILE
    for i in range(2):
        item_at[items + i] = LIST
        item_kv[items + i] = 0

    def tile(i):
        return [rows_of(plan_ref[item_at[i] + g]) for g in range(TILE)]

    def positions(i):
        return pl.ds(pl.multiple_of(item_kv[i] * BLOCK, BLOCK), BLOCK)

    def load(ref, rows):
        return jnp.concatenate([ref[r, :] for r in rows], axis=0)

    def save(ref, rows, value):
        for g, r in enumerate(rows):
            ref[r, :] = value[g * GROUP * HEADS : (g + 1) * GROUP * HEADS]

    def score(i, s_ref):
        s_ref[...] = scores_of(load(qs_ref, tile(i)), kv_ref[positions(i), 0:HD])

    def soften(i, s_ref):
        here = tile(i)
        s, m = s_ref[...], load(m_ref, here)
        fresh = jnp.maximum(m, jnp.max(s, axis=1, keepdims=True))
        shrink = jnp.exp2(m - fresh)
        p = jnp.exp2(s - jnp.concatenate([fresh] * (BLOCK // HD), axis=1)).astype(jnp.bfloat16)
        pv = jnp.dot(p, with_ones(kv_ref[positions(i), HD:]), preferred_element_type=jnp.float32)
        save(m_ref, here, fresh)
        save(l_ref, here, load(l_ref, here) * shrink + pv[:, HD:])
        save(a_ref, here, load(a_ref, here) * shrink + pv[:, :HD])

    @pl.when(items > 0)
    def _():
        score(0, s0_ref)

    def pair(j, c):
        i = j * 2
        score(i + 1, s1_ref)
        soften(i, s0_ref)
        score(i + 2, s0_ref)
        soften(i + 1, s1_ref)
        return c

    lax.fori_loop(0, items // 2, pair, 0)

    @pl.when(items % 2 == 1)
    def _():
        soften(items - 1, s0_ref)

    if number == 3:
        far_ref, far_stat_ref = refs[9:11]
        lane = lax.broadcasted_iota(jnp.int32, (GROUP, 128), 1)
        for g in range(16):
            to = slice(g * GROUP, (g + 1) * GROUP)
            stats = jnp.zeros((GROUP, 128), jnp.float32)
            for h in range(HEADS):
                here = slice(((16 + g) * HEADS + h) * GROUP, ((16 + g) * HEADS + h + 1) * GROUP)
                stats = put_stats(lane, stats, h, m_ref[here, :], l_ref[here, :])
                far_ref[to, h * HD : (h + 1) * HD] = a_ref[here, :].astype(jnp.bfloat16)
            far_stat_ref[to, :] = stats


def fold_call(number, plan, qs, kv, state):
    f32, b16 = jnp.float32, jnp.bfloat16
    shapes = [((STATE_ROWS, HD), f32)] * 3
    if number == 3:
        shapes += [((256, 1024), b16), ((256, 128), f32)]
    operands = [plan, qs, kv, *state]
    wide = (TILE * GROUP * HEADS, BLOCK)
    return pl.pallas_call(
        functools.partial(fold_kernel, number),
        out_shape=[jax.ShapeDtypeStruct(s, d) for s, d in shapes],
        in_specs=[SMEM] + [VMEM] * (len(operands) - 1),
        out_specs=[VMEM] * len(shapes),
        scratch_shapes=[pltpu.SMEM((48,), jnp.int32)] * 2 + [pltpu.VMEM(wide, f32)] * 2,
        input_output_aliases={3: 0, 4: 1, 5: 2},
        compiler_params=pltpu.CompilerParams(vmem_limit_bytes=40 * 2**20),
        cost_estimate=pl.CostEstimate(
            flops=2 * 2560 * kv.shape[0] * 256, bytes_accessed=4 * 2**20, transcendentals=1280 * kv.shape[0]
        ),
        name=f"fold{number}",
    )(*operands)


def join_kernel(len_ref, m_ref, l_ref, a_ref, far_ref, far_stat_ref, out_ref):
    for b in range(2):
        for part in range(2):
            length = len_ref[b] - part * 4 * GROUP
            first = b * BROWS + part * 4 * GROUP

            @pl.when(length > 0)
            def _(b=b, part=part, length=length, first=first):
                for g in range(4):
                    group = b * 8 + part * 4 + g
                    rows = slice(group * GROUP, (group + 1) * GROUP)
                    live = lax.broadcasted_iota(jnp.int32, (GROUP, HD), 0) < length - g * GROUP
                    stats = far_stat_ref[rows, :]
                    for h in range(HEADS):
                        cols = slice(h * HD, (h + 1) * HD)
                        here = slice((group * HEADS + h) * GROUP, (group * HEADS + h + 1) * GROUP)
                        m, far_m = m_ref[here, :], stats[:, h : h + 1]
                        peak = jnp.maximum(m, far_m)
                        w, far_w = jnp.exp2(m - peak), jnp.exp2(far_m - peak)
                        total = w * l_ref[here, :] + far_w * stats[:, HEADS + h : HEADS + h + 1]
                        blended = w * a_ref[here, :] + far_w * far_ref[rows, cols].astype(jnp.float32)
                        out_ref[rows, cols] = jnp.where(live, blended / total, 0.0).astype(jnp.bfloat16)

            @pl.when(length <= 0)
            def _(first=first):
                out_ref[first : first + 4 * GROUP, :] = jnp.zeros((4 * GROUP, HEADS * HD), jnp.bfloat16)


def join(lengths, state, far, far_stat):
    return pl.pallas_call(
        join_kernel,
        out_shape=jax.ShapeDtypeStruct((256, 1024), jnp.bfloat16),
        in_specs=[SMEM] + [VMEM] * 5,
        out_specs=VMEM,
        compiler_params=pltpu.CompilerParams(vmem_limit_bytes=32 * 2**20),
        name="join",
    )(lengths, *state, far, far_stat)


def per_device(queries, answer_kv, prompt_kv, block_prompt, answer_len):
    piece = prompt_kv[0, :, 0, :]
    own_kv = answer_kv[:, 0, :]
    code = block_prompt[:, 0] * 256 + answer_len
    place = jnp.stack([lax.axis_index("grp"), lax.axis_index("ctx") & 1]).astype(jnp.int32)

    even, odd, across = [lax.ppermute(piece, AXES, ring_swap(0, turn)) for turn in ("even", "odd", "across")]
    code_far, q_far = [lax.ppermute(v, AXES, core_swap()) for v in (code, queries)]
    room = jnp.pad(piece, ((0, piece.shape[0]), (0, 0)))
    plan, qs, *state = prep(jnp.concatenate([code, code_far, place]), queries, q_far, own_kv)
    even, odd, across, room, plan, qs, state = lax.optimization_barrier((even, odd, across, room, plan, qs, state))
    held = [lax.dynamic_update_slice(room, even, (piece.shape[0], 0)), jnp.concatenate([odd, across], axis=0)]
    even0, even1 = [lax.ppermute(h, AXES, ring_swap(1, "even")) for h in held]
    odd0, odd1 = [lax.ppermute(h, AXES, ring_swap(1, "odd")) for h in held]
    all_held = jnp.concatenate(held, axis=0)
    across = lax.ppermute(all_held, AXES, ring_swap(1, "across"))
    state = fold_call(0, plan, qs, all_held, state)
    even0, odd1, state = lax.optimization_barrier((even0, odd1, state))
    state = fold_call(1, plan, qs, jnp.concatenate([even0, odd1], axis=0), state)
    odd0, even1, state = lax.optimization_barrier((odd0, even1, state))
    state = fold_call(2, plan, qs, jnp.concatenate([odd0, even1], axis=0), state)
    across, state = lax.optimization_barrier((across, state))
    *state, far, far_stat = fold_call(3, plan, qs, across, state)
    far = lax.ppermute(far, AXES, core_swap())
    far_stat = lax.ppermute(far_stat, AXES, core_swap())
    return join(answer_len, state, far, far_stat)


def solution(mesh):
    placed = (
        P(("ctx", "grp"), "head"),
        P(("ctx", "grp"), "head", None),
        P("grp", "ctx", "head", None),
        P(("ctx", "grp"), None),
        P(("ctx", "grp")),
    )
    return jax.shard_map(
        per_device, mesh=mesh, in_specs=placed, out_specs=P(("ctx", "grp"), "head"), check_vma=False
    )
```

```python
import functools

import jax
import jax.numpy as jnp
import numpy as np
from jax import lax
from jax.experimental import pallas as pl
from jax.experimental.pallas import tpu as pltpu
from jax.sharding import PartitionSpec as P

HD = 128
BROWS = 128
HEADS = 8
BLOCK = 1024
GROUP = 16
TILE = 4
LIST = 8
SPARE = 32
STATE_ROWS = 33 * GROUP * HEADS
SCALE = float(np.log2(np.e) / np.sqrt(HD))
LOW = -1e30
VMEM = pl.BlockSpec(memory_space=pltpu.VMEM)
SMEM = pl.BlockSpec(memory_space=pltpu.SMEM)
AXES = ("ctx", "grp")

TURNS = {"even": lambda i: i ^ 1, "odd": lambda i: 3 - i, "across": lambda i: i ^ 2}


def index_of(x, y, core):
    return ((y * 2 + x % 2) * 2 + core) * 2 + x // 2


def ring_swap(stage, turn):
    pairs = []
    for x in range(4):
        for y in range(4):
            for core in range(2):
                to = (TURNS[turn](x), y) if core == stage else (x, TURNS[turn](y))
                pairs.append((index_of(x, y, core), index_of(*to, core)))
    return pairs


def core_swap():
    return [(index_of(x, y, c), index_of(x, y, 1 - c)) for x in range(4) for y in range(4) for c in range(2)]


def scaled(q):
    wide = q.astype(jnp.float32) * SCALE
    high = wide.astype(jnp.bfloat16)
    low = (wide - high.astype(jnp.float32)).astype(jnp.bfloat16)
    return jnp.concatenate([high, low], axis=1)


def scores_of(q, k):
    return lax.dot_general(
        q, jnp.concatenate([k, k], axis=1), (((1,), (1,)), ((), ())), preferred_element_type=jnp.float32
    )


def with_ones(v):
    return jnp.concatenate([v, jnp.ones_like(v)], axis=1)


def put_stats(lane, stats, h, m, l):
    stats = jnp.where(lane == h, m, stats)
    return jnp.where(lane == HEADS + h, l, stats)


def make_plan(meta_ref, plan_ref):
    offset = jnp.int32(0)
    for want in range(2):
        count = jnp.int32(0)
        for b in range(4):
            code = meta_ref[b]
            live = ((code & 255) + (GROUP - 1)) // GROUP
            live = jnp.where((code >> 8) == (meta_ref[4] ^ want), live, 0)

            def add(i, c, b=b, at=LIST + offset + count):
                plan_ref[at + i] = b * 8 + i
                return c

            lax.fori_loop(0, live, add, 0)
            count = count + live
        tiles = (count + (TILE - 1)) // TILE
        for i in range(TILE - 1):
            plan_ref[LIST + offset + count + i] = SPARE
        plan_ref[want] = tiles
        offset = offset + tiles * TILE
    plan_ref[2] = meta_ref[5]


def rows_of(group):
    return pl.ds(pl.multiple_of(group * (GROUP * HEADS), GROUP * HEADS), GROUP * HEADS)


def prep_kernel(meta_ref, q_ref, far_ref, kv_ref, plan_ref, qs_ref, m_ref, l_ref, a_ref):
    make_plan(meta_ref, plan_ref)
    shape = (HEADS * BROWS, BROWS)
    row = lax.broadcasted_iota(jnp.int32, shape, 0) % BROWS
    causal = row >= lax.broadcasted_iota(jnp.int32, shape, 1)
    for b in range(2):
        rows = slice(b * BROWS, (b + 1) * BROWS)
        q = scaled(jnp.concatenate([q_ref[rows, h * HD : (h + 1) * HD] for h in range(HEADS)], axis=0))
        s = jnp.where(causal, scores_of(q, kv_ref[rows, 0:HD]), LOW)
        m = jnp.max(s, axis=1, keepdims=True)
        p = jnp.exp2(s - m)
        pv = jnp.dot(p.astype(jnp.bfloat16), with_ones(kv_ref[rows, HD:]), preferred_element_type=jnp.float32)
        m = jnp.broadcast_to(m, (HEADS * BROWS, HD))
        for g in range(8):
            for h in range(HEADS):
                here = slice(((b * 8 + g) * HEADS + h) * GROUP, ((b * 8 + g) * HEADS + h + 1) * GROUP)
                part = slice(h * BROWS + g * GROUP, h * BROWS + (g + 1) * GROUP)
                qs_ref[here, :] = q[part]
                m_ref[here, :] = m[part]
                l_ref[here, :] = pv[part, HD:]
                a_ref[here, :] = pv[part, :HD]
    for g in range(16):
        for h in range(HEADS):
            here = slice(((16 + g) * HEADS + h) * GROUP, ((16 + g) * HEADS + h + 1) * GROUP)
            qs_ref[here, :] = scaled(far_ref[g * GROUP : (g + 1) * GROUP, h * HD : (h + 1) * HD])
    rest = slice(16 * GROUP * HEADS, STATE_ROWS)
    size = (STATE_ROWS - 16 * GROUP * HEADS, HD)
    m_ref[rest, :] = jnp.full(size, LOW, jnp.float32)
    l_ref[rest, :] = jnp.zeros(size, jnp.float32)
    a_ref[rest, :] = jnp.zeros(size, jnp.float32)
    qs_ref[SPARE * GROUP * HEADS : STATE_ROWS, :] = jnp.zeros((GROUP * HEADS, 2 * HD), jnp.bfloat16)


def prep(meta, q, far, kv):
    return pl.pallas_call(
        prep_kernel,
        out_shape=[
            jax.ShapeDtypeStruct((64,), jnp.int32),
            jax.ShapeDtypeStruct((STATE_ROWS, 2 * HD), jnp.bfloat16),
        ]
        + [jax.ShapeDtypeStruct((STATE_ROWS, HD), jnp.float32)] * 3,
        in_specs=[SMEM] + [VMEM] * 3,
        out_specs=[SMEM] + [VMEM] * 4,
        compiler_params=pltpu.CompilerParams(vmem_limit_bytes=40 * 2**20),
        cost_estimate=pl.CostEstimate(flops=2 * 2048 * 128 * 512, bytes_accessed=3 * 2**20, transcendentals=2048 * 128),
        name="prep",
    )(meta, q, far, kv)


def fold_kernel(number, *refs):
    refs = list(refs)
    plan_ref, qs_ref, kv_ref = refs[:3]
    m_ref, l_ref, a_ref = refs[6:9]
    item_at, item_kv, s0_ref, s1_ref = refs[-4:]
    core = plan_ref[2]

    items, first = jnp.int32(0), jnp.int32(LIST)
    for want in range(2):
        tiles = plan_ref[want]
        most = 1
        if number == 0:
            blocks, many = (0,), 1 - want
        elif number == 1:
            blocks, many = (1,), jnp.where((want ^ core) == 1, 1, 0)
        elif number == 2:
            blocks, many, most = (jnp.where(core == 0, want, 2 * want), jnp.where(core == 0, 2 + want, 2 * want + 1)), 2, 2
        else:
            blocks, many, most = (jnp.where(core == 0, want, 0), 1), jnp.where(core == 0, 1, 2 * want), 2

        def add(t, c, first=first, blocks=blocks, many=many, most=most, items=items):
            for i in range(most):

                @pl.when(i < many)
                def _(i=i):
                    item_at[items + t * many + i] = first + t * TILE
                    item_kv[items + t * many + i] = blocks[i]

            return c

        lax.fori_loop(0, tiles, add, 0)
        items = items + tiles * many
        first = first + tiles * TILE
    for i in range(2):
        item_at[items + i] = LIST
        item_kv[items + i] = 0

    def tile(i):
        return [rows_of(plan_ref[item_at[i] + g]) for g in range(TILE)]

    def positions(i):
        return pl.ds(pl.multiple_of(item_kv[i] * BLOCK, BLOCK), BLOCK)

    def load(ref, rows):
        return jnp.concatenate([ref[r, :] for r in rows], axis=0)

    def save(ref, rows, value):
        for g, r in enumerate(rows):
            ref[r, :] = value[g * GROUP * HEADS : (g + 1) * GROUP * HEADS]

    def score(i, s_ref):
        s_ref[...] = scores_of(load(qs_ref, tile(i)), kv_ref[positions(i), 0:HD])

    def soften(i, s_ref):
        here = tile(i)
        s, m = s_ref[...], load(m_ref, here)
        fresh = jnp.maximum(m, jnp.max(s, axis=1, keepdims=True))
        shrink = jnp.exp2(m - fresh)
        p = jnp.exp2(s - jnp.concatenate([fresh] * (BLOCK // HD), axis=1)).astype(jnp.bfloat16)
        pv = jnp.dot(p, with_ones(kv_ref[positions(i), HD:]), preferred_element_type=jnp.float32)
        save(m_ref, here, fresh)
        save(l_ref, here, load(l_ref, here) * shrink + pv[:, HD:])
        save(a_ref, here, load(a_ref, here) * shrink + pv[:, :HD])

    @pl.when(items > 0)
    def _():
        score(0, s0_ref)

    def pair(j, c):
        i = j * 2
        score(i + 1, s1_ref)
        soften(i, s0_ref)
        score(i + 2, s0_ref)
        soften(i + 1, s1_ref)
        return c

    lax.fori_loop(0, items // 2, pair, 0)

    @pl.when(items % 2 == 1)
    def _():
        soften(items - 1, s0_ref)

    if number == 3:
        far_ref, far_stat_ref = refs[9:11]
        lane = lax.broadcasted_iota(jnp.int32, (GROUP, 128), 1)
        for g in range(16):
            to = slice(g * GROUP, (g + 1) * GROUP)
            stats = jnp.zeros((GROUP, 128), jnp.float32)
            for h in range(HEADS):
                here = slice(((16 + g) * HEADS + h) * GROUP, ((16 + g) * HEADS + h + 1) * GROUP)
                stats = put_stats(lane, stats, h, m_ref[here, :], l_ref[here, :])
                far_ref[to, h * HD : (h + 1) * HD] = a_ref[here, :].astype(jnp.bfloat16)
            far_stat_ref[to, :] = stats


def fold_call(number, plan, qs, kv, state):
    f32, b16 = jnp.float32, jnp.bfloat16
    shapes = [((STATE_ROWS, HD), f32)] * 3
    if number == 3:
        shapes += [((256, 1024), b16), ((256, 128), f32)]
    operands = [plan, qs, kv, *state]
    wide = (TILE * GROUP * HEADS, BLOCK)
    return pl.pallas_call(
        functools.partial(fold_kernel, number),
        out_shape=[jax.ShapeDtypeStruct(s, d) for s, d in shapes],
        in_specs=[SMEM] + [VMEM] * (len(operands) - 1),
        out_specs=[VMEM] * len(shapes),
        scratch_shapes=[pltpu.SMEM((48,), jnp.int32)] * 2 + [pltpu.VMEM(wide, f32)] * 2,
        input_output_aliases={3: 0, 4: 1, 5: 2},
        compiler_params=pltpu.CompilerParams(vmem_limit_bytes=40 * 2**20),
        cost_estimate=pl.CostEstimate(
            flops=2 * 2560 * kv.shape[0] * 256, bytes_accessed=4 * 2**20, transcendentals=1280 * kv.shape[0]
        ),
        name=f"fold{number}",
    )(*operands)


def join_kernel(len_ref, m_ref, l_ref, a_ref, far_ref, far_stat_ref, out_hbm, out_ref, sems):
    copies = []
    for b in range(2):
        for part in range(2):
            length = len_ref[b] - part * 4 * GROUP
            first = b * BROWS + part * 4 * GROUP

            @pl.when(length > 0)
            def _(b=b, part=part, length=length, first=first):
                for g in range(4):
                    group = b * 8 + part * 4 + g
                    rows = slice(group * GROUP, (group + 1) * GROUP)
                    live = lax.broadcasted_iota(jnp.int32, (GROUP, HD), 0) < length - g * GROUP
                    stats = far_stat_ref[rows, :]
                    for h in range(HEADS):
                        cols = slice(h * HD, (h + 1) * HD)
                        here = slice((group * HEADS + h) * GROUP, (group * HEADS + h + 1) * GROUP)
                        m, far_m = m_ref[here, :], stats[:, h : h + 1]
                        peak = jnp.maximum(m, far_m)
                        w, far_w = jnp.exp2(m - peak), jnp.exp2(far_m - peak)
                        total = w * l_ref[here, :] + far_w * stats[:, HEADS + h : HEADS + h + 1]
                        blended = w * a_ref[here, :] + far_w * far_ref[rows, cols].astype(jnp.float32)
                        out_ref[rows, cols] = jnp.where(live, blended / total, 0.0).astype(jnp.bfloat16)

            @pl.when(length <= 0)
            def _(first=first):
                out_ref[first : first + 4 * GROUP, :] = jnp.zeros((4 * GROUP, HEADS * HD), jnp.bfloat16)

            rows = pl.ds(first, 4 * GROUP)
            copy = pltpu.make_async_copy(out_ref.at[rows], out_hbm.at[rows], sems.at[b * 2 + part])
            copy.start()
            copies.append(copy)
    for copy in copies:
        copy.wait()


def join(lengths, state, far, far_stat):
    return pl.pallas_call(
        join_kernel,
        out_shape=jax.ShapeDtypeStruct((256, 1024), jnp.bfloat16),
        in_specs=[SMEM] + [VMEM] * 5,
        out_specs=pl.BlockSpec(memory_space=pl.ANY),
        scratch_shapes=[pltpu.VMEM((256, 1024), jnp.bfloat16), pltpu.SemaphoreType.DMA((4,))],
        compiler_params=pltpu.CompilerParams(vmem_limit_bytes=32 * 2**20),
        name="join",
    )(lengths, *state, far, far_stat)


def per_device(queries, answer_kv, prompt_kv, block_prompt, answer_len):
    piece = prompt_kv[0, :, 0, :]
    own_kv = answer_kv[:, 0, :]
    code = block_prompt[:, 0] * 256 + answer_len
    place = jnp.stack([lax.axis_index("grp"), lax.axis_index("ctx") & 1]).astype(jnp.int32)

    even, odd, across = [lax.ppermute(piece, AXES, ring_swap(0, turn)) for turn in ("even", "odd", "across")]
    code_far, q_far = [lax.ppermute(v, AXES, core_swap()) for v in (code, queries)]
    room = jnp.pad(piece, ((0, piece.shape[0]), (0, 0)))
    plan, qs, *state = prep(jnp.concatenate([code, code_far, place]), queries, q_far, own_kv)
    even, odd, across, room, plan, qs, state = lax.optimization_barrier((even, odd, across, room, plan, qs, state))
    held = [lax.dynamic_update_slice(room, even, (piece.shape[0], 0)), jnp.concatenate([odd, across], axis=0)]
    all_held = jnp.concatenate(held, axis=0)
    from_even = lax.ppermute(all_held, AXES, ring_swap(1, "even"))
    from_odd = lax.ppermute(all_held, AXES, ring_swap(1, "odd"))
    state = fold_call(0, plan, qs, all_held, state)
    from_even, from_odd, state = lax.optimization_barrier((from_even, from_odd, state))
    last = [
        lax.ppermute(from_even[:BLOCK], AXES, ring_swap(1, "odd")),
        lax.ppermute(from_odd[BLOCK:], AXES, ring_swap(1, "even")),
    ]
    state = fold_call(1, plan, qs, all_held, state)
    state = fold_call(2, plan, qs, jnp.concatenate([from_even, from_odd], axis=0), state)
    last, state = lax.optimization_barrier((last, state))
    *state, far, far_stat = fold_call(3, plan, qs, jnp.concatenate(last, axis=0), state)
    far = lax.ppermute(far, AXES, core_swap())
    far_stat = lax.ppermute(far_stat, AXES, core_swap())
    return join(answer_len, state, far, far_stat)


def solution(mesh):
    placed = (
        P(("ctx", "grp"), "head"),
        P(("ctx", "grp"), "head", None),
        P("grp", "ctx", "head", None),
        P(("ctx", "grp"), None),
        P(("ctx", "grp")),
    )
    return jax.shard_map(
        per_device, mesh=mesh, in_specs=placed, out_specs=P(("ctx", "grp"), "head"), check_vma=False
    )
```

```python
import functools

import jax
import jax.numpy as jnp
import numpy as np
from jax import lax
from jax.experimental import pallas as pl
from jax.experimental.pallas import tpu as pltpu
from jax.sharding import PartitionSpec as P

HD = 128
BROWS = 128
HEADS = 8
BLOCK = 1024
GROUP = 16
TILE = 4
LIST = 8
SPARE = 32
STATE_ROWS = 33 * GROUP * HEADS
SCALE = float(np.log2(np.e) / np.sqrt(HD))
LOW = -1e30
VMEM = pl.BlockSpec(memory_space=pltpu.VMEM)
SMEM = pl.BlockSpec(memory_space=pltpu.SMEM)
AXES = ("ctx", "grp")

TURNS = {"even": lambda i: i ^ 1, "odd": lambda i: 3 - i, "across": lambda i: i ^ 2}


def index_of(x, y, core):
    return ((y * 2 + x % 2) * 2 + core) * 2 + x // 2


def ring_swap(stage, turn):
    pairs = []
    for x in range(4):
        for y in range(4):
            for core in range(2):
                to = (TURNS[turn](x), y) if core == stage else (x, TURNS[turn](y))
                pairs.append((index_of(x, y, core), index_of(*to, core)))
    return pairs


def core_swap():
    return [(index_of(x, y, c), index_of(x, y, 1 - c)) for x in range(4) for y in range(4) for c in range(2)]


def scaled(q):
    wide = q.astype(jnp.float32) * SCALE
    high = wide.astype(jnp.bfloat16)
    low = (wide - high.astype(jnp.float32)).astype(jnp.bfloat16)
    return jnp.concatenate([high, low], axis=1)


def scores_of(q, k):
    return lax.dot_general(
        q, jnp.concatenate([k, k], axis=1), (((1,), (1,)), ((), ())), preferred_element_type=jnp.float32
    )


def with_ones(v):
    return jnp.concatenate([v, jnp.ones_like(v)], axis=1)


def put_stats(lane, stats, h, m, l):
    stats = jnp.where(lane == h, m, stats)
    return jnp.where(lane == HEADS + h, l, stats)


def make_plan(meta_ref, plan_ref):
    offset = jnp.int32(0)
    for want in range(2):
        count = jnp.int32(0)
        for b in (2, 3, 0, 1):
            code = meta_ref[b]
            live = ((code & 255) + (GROUP - 1)) // GROUP
            live = jnp.where((code >> 8) == (meta_ref[4] ^ want), live, 0)

            def add(i, c, b=b, at=LIST + offset + count):
                plan_ref[at + i] = b * 8 + i
                return c

            lax.fori_loop(0, live, add, 0)
            count = count + live
            if b == 3:
                plan_ref[3 + want] = (count + (TILE - 1)) // TILE
        tiles = (count + (TILE - 1)) // TILE
        for i in range(TILE - 1):
            plan_ref[LIST + offset + count + i] = SPARE
        plan_ref[want] = tiles
        offset = offset + tiles * TILE
    plan_ref[2] = meta_ref[5]


def rows_of(group):
    return pl.ds(pl.multiple_of(group * (GROUP * HEADS), GROUP * HEADS), GROUP * HEADS)


def prep_kernel(meta_ref, q_ref, far_ref, kv_ref, plan_ref, qs_ref, m_ref, l_ref, a_ref):
    make_plan(meta_ref, plan_ref)
    shape = (HEADS * BROWS, BROWS)
    row = lax.broadcasted_iota(jnp.int32, shape, 0) % BROWS
    causal = row >= lax.broadcasted_iota(jnp.int32, shape, 1)
    for b in range(2):
        rows = slice(b * BROWS, (b + 1) * BROWS)
        q = scaled(jnp.concatenate([q_ref[rows, h * HD : (h + 1) * HD] for h in range(HEADS)], axis=0))
        s = jnp.where(causal, scores_of(q, kv_ref[rows, 0:HD]), LOW)
        m = jnp.max(s, axis=1, keepdims=True)
        p = jnp.exp2(s - m)
        pv = jnp.dot(p.astype(jnp.bfloat16), with_ones(kv_ref[rows, HD:]), preferred_element_type=jnp.float32)
        m = jnp.broadcast_to(m, (HEADS * BROWS, HD))
        for g in range(8):
            for h in range(HEADS):
                here = slice(((b * 8 + g) * HEADS + h) * GROUP, ((b * 8 + g) * HEADS + h + 1) * GROUP)
                part = slice(h * BROWS + g * GROUP, h * BROWS + (g + 1) * GROUP)
                qs_ref[here, :] = q[part]
                m_ref[here, :] = m[part]
                l_ref[here, :] = pv[part, HD:]
                a_ref[here, :] = pv[part, :HD]
    for g in range(16):
        for h in range(HEADS):
            here = slice(((16 + g) * HEADS + h) * GROUP, ((16 + g) * HEADS + h + 1) * GROUP)
            qs_ref[here, :] = scaled(far_ref[g * GROUP : (g + 1) * GROUP, h * HD : (h + 1) * HD])
    rest = slice(16 * GROUP * HEADS, STATE_ROWS)
    size = (STATE_ROWS - 16 * GROUP * HEADS, HD)
    m_ref[rest, :] = jnp.full(size, LOW, jnp.float32)
    l_ref[rest, :] = jnp.zeros(size, jnp.float32)
    a_ref[rest, :] = jnp.zeros(size, jnp.float32)
    qs_ref[SPARE * GROUP * HEADS : STATE_ROWS, :] = jnp.zeros((GROUP * HEADS, 2 * HD), jnp.bfloat16)


def prep(meta, q, far, kv):
    return pl.pallas_call(
        prep_kernel,
        out_shape=[
            jax.ShapeDtypeStruct((64,), jnp.int32),
            jax.ShapeDtypeStruct((STATE_ROWS, 2 * HD), jnp.bfloat16),
        ]
        + [jax.ShapeDtypeStruct((STATE_ROWS, HD), jnp.float32)] * 3,
        in_specs=[SMEM] + [VMEM] * 3,
        out_specs=[SMEM] + [VMEM] * 4,
        compiler_params=pltpu.CompilerParams(vmem_limit_bytes=40 * 2**20),
        cost_estimate=pl.CostEstimate(flops=2 * 2048 * 128 * 512, bytes_accessed=3 * 2**20, transcendentals=2048 * 128),
        name="prep",
    )(meta, q, far, kv)


def fold_kernel(number, *refs):
    refs = list(refs)
    plan_ref, qs_ref, kv_ref = refs[:3]
    m_ref, l_ref, a_ref = refs[6:9]
    item_at, item_kv, s0_ref, s1_ref = refs[-4:]
    core = plan_ref[2]

    items, first = jnp.int32(0), jnp.int32(LIST)
    for want in range(2):
        tiles, far_tiles = plan_ref[want], plan_ref[3 + want]
        start = far_tiles if number == 4 else 0
        used = (far_tiles if number == 3 else tiles) - start
        if number == 1:
            blocks, many = (want, 0), 1
        elif number == 2:
            blocks, many = (want ^ core, 0), 1
        else:
            blocks = (jnp.where(core == 0, want, 0), 1)
            many = jnp.where(core == 0, 1, 2 if (want == 0) == (number == 0) else 0)

        def add(t, c, first=first, blocks=blocks, many=many, items=items, start=start):
            for i in range(1 if number in (1, 2) else 2):

                @pl.when(i < many)
                def _(i=i):
                    item_at[items + t * many + i] = first + (start + t) * TILE
                    item_kv[items + t * many + i] = blocks[i]

            return c

        lax.fori_loop(0, used, add, 0)
        items = items + used * many
        first = first + tiles * TILE
    for i in range(2):
        item_at[items + i] = LIST
        item_kv[items + i] = 0

    def tile(i):
        return [rows_of(plan_ref[item_at[i] + g]) for g in range(TILE)]

    def positions(i):
        return pl.ds(pl.multiple_of(item_kv[i] * BLOCK, BLOCK), BLOCK)

    def load(ref, rows):
        return jnp.concatenate([ref[r, :] for r in rows], axis=0)

    def save(ref, rows, value):
        for g, r in enumerate(rows):
            ref[r, :] = value[g * GROUP * HEADS : (g + 1) * GROUP * HEADS]

    def score(i, s_ref):
        s_ref[...] = scores_of(load(qs_ref, tile(i)), kv_ref[positions(i), 0:HD])

    def soften(i, s_ref):
        here = tile(i)
        s, m = s_ref[...], load(m_ref, here)
        fresh = jnp.maximum(m, jnp.max(s, axis=1, keepdims=True))
        shrink = jnp.exp2(m - fresh)
        p = jnp.exp2(s - jnp.concatenate([fresh] * (BLOCK // HD), axis=1)).astype(jnp.bfloat16)
        pv = jnp.dot(p, with_ones(kv_ref[positions(i), HD:]), preferred_element_type=jnp.float32)
        save(m_ref, here, fresh)
        save(l_ref, here, load(l_ref, here) * shrink + pv[:, HD:])
        save(a_ref, here, load(a_ref, here) * shrink + pv[:, :HD])

    @pl.when(items > 0)
    def _():
        score(0, s0_ref)

    def pair(j, c):
        i = j * 2
        score(i + 1, s1_ref)
        soften(i, s0_ref)
        score(i + 2, s0_ref)
        soften(i + 1, s1_ref)
        return c

    lax.fori_loop(0, items // 2, pair, 0)

    @pl.when(items % 2 == 1)
    def _():
        soften(items - 1, s0_ref)

    if number == 3:
        far_ref, far_stat_ref = refs[9:11]
        lane = lax.broadcasted_iota(jnp.int32, (GROUP, 128), 1)
        for g in range(16):
            to = slice(g * GROUP, (g + 1) * GROUP)
            stats = jnp.zeros((GROUP, 128), jnp.float32)
            for h in range(HEADS):
                here = slice(((16 + g) * HEADS + h) * GROUP, ((16 + g) * HEADS + h + 1) * GROUP)
                stats = put_stats(lane, stats, h, m_ref[here, :], l_ref[here, :])
                far_ref[to, h * HD : (h + 1) * HD] = a_ref[here, :].astype(jnp.bfloat16)
            far_stat_ref[to, :] = stats


def fold_call(number, plan, qs, kv, state):
    f32, b16 = jnp.float32, jnp.bfloat16
    shapes = [((STATE_ROWS, HD), f32)] * 3
    if number == 3:
        shapes += [((256, 1024), b16), ((256, 128), f32)]
    operands = [plan, qs, kv, *state]
    wide = (TILE * GROUP * HEADS, BLOCK)
    return pl.pallas_call(
        functools.partial(fold_kernel, number),
        out_shape=[jax.ShapeDtypeStruct(s, d) for s, d in shapes],
        in_specs=[SMEM] + [VMEM] * (len(operands) - 1),
        out_specs=[VMEM] * len(shapes),
        scratch_shapes=[pltpu.SMEM((48,), jnp.int32)] * 2 + [pltpu.VMEM(wide, f32)] * 2,
        input_output_aliases={3: 0, 4: 1, 5: 2},
        compiler_params=pltpu.CompilerParams(vmem_limit_bytes=40 * 2**20),
        cost_estimate=pl.CostEstimate(
            flops=2 * 2560 * kv.shape[0] * 256, bytes_accessed=4 * 2**20, transcendentals=1280 * kv.shape[0]
        ),
        name=f"fold{number}",
    )(*operands)


def join_kernel(len_ref, m_ref, l_ref, a_ref, far_ref, far_stat_ref, out_ref):
    for b in range(2):
        for part in range(2):
            length = len_ref[b] - part * 4 * GROUP
            first = b * BROWS + part * 4 * GROUP

            @pl.when(length > 0)
            def _(b=b, part=part, length=length, first=first):
                for g in range(4):
                    group = b * 8 + part * 4 + g
                    rows = slice(group * GROUP, (group + 1) * GROUP)
                    live = lax.broadcasted_iota(jnp.int32, (GROUP, HD), 0) < length - g * GROUP
                    stats = far_stat_ref[rows, :]
                    for h in range(HEADS):
                        cols = slice(h * HD, (h + 1) * HD)
                        here = slice((group * HEADS + h) * GROUP, (group * HEADS + h + 1) * GROUP)
                        m, far_m = m_ref[here, :], stats[:, h : h + 1]
                        peak = jnp.maximum(m, far_m)
                        w, far_w = jnp.exp2(m - peak), jnp.exp2(far_m - peak)
                        total = w * l_ref[here, :] + far_w * stats[:, HEADS + h : HEADS + h + 1]
                        blended = w * a_ref[here, :] + far_w * far_ref[rows, cols].astype(jnp.float32)
                        out_ref[rows, cols] = jnp.where(live, blended / total, 0.0).astype(jnp.bfloat16)

            @pl.when(length <= 0)
            def _(first=first):
                out_ref[first : first + 4 * GROUP, :] = jnp.zeros((4 * GROUP, HEADS * HD), jnp.bfloat16)


def join(lengths, state, far, far_stat):
    return pl.pallas_call(
        join_kernel,
        out_shape=jax.ShapeDtypeStruct((256, 1024), jnp.bfloat16),
        in_specs=[SMEM] + [VMEM] * 5,
        out_specs=VMEM,
        compiler_params=pltpu.CompilerParams(vmem_limit_bytes=32 * 2**20),
        name="join",
    )(lengths, *state, far, far_stat)


def per_device(queries, answer_kv, prompt_kv, block_prompt, answer_len):
    piece = prompt_kv[0, :, 0, :]
    own_kv = answer_kv[:, 0, :]
    code = block_prompt[:, 0] * 256 + answer_len
    place = jnp.stack([lax.axis_index("grp"), lax.axis_index("ctx") & 1]).astype(jnp.int32)

    even, odd, across = [lax.ppermute(piece, AXES, ring_swap(0, turn)) for turn in ("even", "odd", "across")]
    code_far, q_far = [lax.ppermute(v, AXES, core_swap()) for v in (code, queries)]
    room = jnp.pad(piece, ((0, piece.shape[0]), (0, 0)))
    plan, qs, *state = prep(jnp.concatenate([code, code_far, place]), queries, q_far, own_kv)
    even, odd, across, room, plan, qs, state = lax.optimization_barrier((even, odd, across, room, plan, qs, state))
    held = [lax.dynamic_update_slice(room, even, (piece.shape[0], 0)), jnp.concatenate([odd, across], axis=0)]
    even0, even1 = [lax.ppermute(h, AXES, ring_swap(1, "even")) for h in held]
    odd0, odd1 = [lax.ppermute(h, AXES, ring_swap(1, "odd")) for h in held]
    all_held = jnp.concatenate(held, axis=0)
    across = lax.ppermute(all_held, AXES, ring_swap(1, "across"))
    state = fold_call(0, plan, qs, all_held, state)
    even0, odd1, state = lax.optimization_barrier((even0, odd1, state))
    state = fold_call(1, plan, qs, jnp.concatenate([even0, odd1], axis=0), state)
    odd0, even1, state = lax.optimization_barrier((odd0, even1, state))
    state = fold_call(2, plan, qs, jnp.concatenate([odd0, even1], axis=0), state)
    across, state = lax.optimization_barrier((across, state))
    *state, far, far_stat = fold_call(3, plan, qs, across, state)
    far = lax.ppermute(far, AXES, core_swap())
    far_stat = lax.ppermute(far_stat, AXES, core_swap())
    state = fold_call(4, plan, qs, across, state)
    return join(answer_len, state, far, far_stat)


def solution(mesh):
    placed = (
        P(("ctx", "grp"), "head"),
        P(("ctx", "grp"), "head", None),
        P("grp", "ctx", "head", None),
        P(("ctx", "grp"), None),
        P(("ctx", "grp")),
    )
    return jax.shard_map(
        per_device, mesh=mesh, in_specs=placed, out_specs=P(("ctx", "grp"), "head"), check_vma=False
    )
```

```python
import functools

import jax
import jax.numpy as jnp
import numpy as np
from jax import lax
from jax.experimental import pallas as pl
from jax.experimental.pallas import tpu as pltpu
from jax.sharding import PartitionSpec as P

HD = 128
BROWS = 128
HEADS = 8
BLOCK = 1024
GROUP = 16
TILE = 4
LIST = 8
SPARE = 32
STATE_ROWS = 33 * GROUP * HEADS
SCALE = float(np.log2(np.e) / np.sqrt(HD))
LOW = -1e30
VMEM = pl.BlockSpec(memory_space=pltpu.VMEM)
SMEM = pl.BlockSpec(memory_space=pltpu.SMEM)
AXES = ("ctx", "grp")

TURNS = {"even": lambda i: i ^ 1, "odd": lambda i: 3 - i, "across": lambda i: i ^ 2}


def index_of(x, y, core):
    return ((y * 2 + x % 2) * 2 + core) * 2 + x // 2


def ring_swap(stage, turn):
    pairs = []
    for x in range(4):
        for y in range(4):
            for core in range(2):
                to = (TURNS[turn](x), y) if core == stage else (x, TURNS[turn](y))
                pairs.append((index_of(x, y, core), index_of(*to, core)))
    return pairs


def core_swap():
    return [(index_of(x, y, c), index_of(x, y, 1 - c)) for x in range(4) for y in range(4) for c in range(2)]


def scaled(q):
    wide = q.astype(jnp.float32) * SCALE
    high = wide.astype(jnp.bfloat16)
    low = (wide - high.astype(jnp.float32)).astype(jnp.bfloat16)
    return jnp.concatenate([high, low], axis=1)


def scores_of(q, k):
    return lax.dot_general(
        q, jnp.concatenate([k, k], axis=1), (((1,), (1,)), ((), ())), preferred_element_type=jnp.float32
    )


def with_ones(v):
    return jnp.concatenate([v, jnp.ones_like(v)], axis=1)


def put_stats(lane, stats, h, m, l):
    stats = jnp.where(lane == h, m, stats)
    return jnp.where(lane == HEADS + h, l, stats)


def make_plan(meta_ref, plan_ref):
    offset = jnp.int32(0)
    for want in range(2):
        count = jnp.int32(0)
        for b in (2, 3, 0, 1):
            code = meta_ref[b]
            live = ((code & 255) + (GROUP - 1)) // GROUP
            live = jnp.where((code >> 8) == (meta_ref[4] ^ want), live, 0)

            def add(i, c, b=b, at=LIST + offset + count):
                plan_ref[at + i] = b * 8 + i
                return c

            lax.fori_loop(0, live, add, 0)
            count = count + live
            if b == 3:
                plan_ref[3 + want] = (count + (TILE - 1)) // TILE
        tiles = (count + (TILE - 1)) // TILE
        for i in range(TILE - 1):
            plan_ref[LIST + offset + count + i] = SPARE
        plan_ref[want] = tiles
        offset = offset + tiles * TILE
    plan_ref[2] = meta_ref[5]


def rows_of(group):
    return pl.ds(pl.multiple_of(group * (GROUP * HEADS), GROUP * HEADS), GROUP * HEADS)


def prep_kernel(meta_ref, q_ref, far_ref, kv_ref, plan_ref, qs_ref, m_ref, l_ref, a_ref):
    make_plan(meta_ref, plan_ref)
    shape = (HEADS * BROWS, BROWS)
    row = lax.broadcasted_iota(jnp.int32, shape, 0) % BROWS
    causal = row >= lax.broadcasted_iota(jnp.int32, shape, 1)
    for b in range(2):
        rows = slice(b * BROWS, (b + 1) * BROWS)
        q = scaled(jnp.concatenate([q_ref[rows, h * HD : (h + 1) * HD] for h in range(HEADS)], axis=0))
        s = jnp.where(causal, scores_of(q, kv_ref[rows, 0:HD]), LOW)
        m = jnp.max(s, axis=1, keepdims=True)
        p = jnp.exp2(s - m)
        pv = jnp.dot(p.astype(jnp.bfloat16), with_ones(kv_ref[rows, HD:]), preferred_element_type=jnp.float32)
        m = jnp.broadcast_to(m, (HEADS * BROWS, HD))
        for g in range(8):
            for h in range(HEADS):
                here = slice(((b * 8 + g) * HEADS + h) * GROUP, ((b * 8 + g) * HEADS + h + 1) * GROUP)
                part = slice(h * BROWS + g * GROUP, h * BROWS + (g + 1) * GROUP)
                qs_ref[here, :] = q[part]
                m_ref[here, :] = m[part]
                l_ref[here, :] = pv[part, HD:]
                a_ref[here, :] = pv[part, :HD]
    for g in range(16):
        for h in range(HEADS):
            here = slice(((16 + g) * HEADS + h) * GROUP, ((16 + g) * HEADS + h + 1) * GROUP)
            qs_ref[here, :] = scaled(far_ref[g * GROUP : (g + 1) * GROUP, h * HD : (h + 1) * HD])
    rest = slice(16 * GROUP * HEADS, STATE_ROWS)
    size = (STATE_ROWS - 16 * GROUP * HEADS, HD)
    m_ref[rest, :] = jnp.full(size, LOW, jnp.float32)
    l_ref[rest, :] = jnp.zeros(size, jnp.float32)
    a_ref[rest, :] = jnp.zeros(size, jnp.float32)
    qs_ref[SPARE * GROUP * HEADS : STATE_ROWS, :] = jnp.zeros((GROUP * HEADS, 2 * HD), jnp.bfloat16)


def prep(meta, q, far, kv):
    return pl.pallas_call(
        prep_kernel,
        out_shape=[
            jax.ShapeDtypeStruct((64,), jnp.int32),
            jax.ShapeDtypeStruct((STATE_ROWS, 2 * HD), jnp.bfloat16),
        ]
        + [jax.ShapeDtypeStruct((STATE_ROWS, HD), jnp.float32)] * 3,
        in_specs=[SMEM] + [VMEM] * 3,
        out_specs=[SMEM] + [VMEM] * 4,
        compiler_params=pltpu.CompilerParams(vmem_limit_bytes=40 * 2**20),
        cost_estimate=pl.CostEstimate(flops=2 * 2048 * 128 * 512, bytes_accessed=3 * 2**20, transcendentals=2048 * 128),
        name="prep",
    )(meta, q, far, kv)


def fold_kernel(number, *refs):
    refs = list(refs)
    plan_ref, qs_ref, kv_ref = refs[:3]
    m_ref, l_ref, a_ref = refs[6:9]
    item_at, item_kv, s0_ref, s1_ref = refs[-4:]
    core = plan_ref[2]

    items, first = jnp.int32(0), jnp.int32(LIST)
    for want in range(2):
        tiles, far_tiles = plan_ref[want], plan_ref[3 + want]
        start = far_tiles if number == 4 else 0
        used = (far_tiles if number == 3 else tiles) - start
        if number == 1:
            blocks, many = (want, 0), 1
        elif number == 2:
            blocks, many = (want ^ core, 0), 1
        else:
            blocks = (jnp.where(core == 0, want, 0), 1)
            many = jnp.where(core == 0, 1, 2 if (want == 0) == (number == 0) else 0)

        def add(t, c, first=first, blocks=blocks, many=many, items=items, start=start):
            for i in range(1 if number in (1, 2) else 2):

                @pl.when(i < many)
                def _(i=i):
                    item_at[items + t * many + i] = first + (start + t) * TILE
                    item_kv[items + t * many + i] = blocks[i]

            return c

        lax.fori_loop(0, used, add, 0)
        items = items + used * many
        first = first + tiles * TILE
    for i in range(2):
        item_at[items + i] = LIST
        item_kv[items + i] = 0

    def tile(i):
        return [rows_of(plan_ref[item_at[i] + g]) for g in range(TILE)]

    def positions(i):
        return pl.ds(pl.multiple_of(item_kv[i] * BLOCK, BLOCK), BLOCK)

    def load(ref, rows):
        return jnp.concatenate([ref[r, :] for r in rows], axis=0)

    def save(ref, rows, value):
        for g, r in enumerate(rows):
            ref[r, :] = value[g * GROUP * HEADS : (g + 1) * GROUP * HEADS]

    def score(i, s_ref):
        s_ref[...] = scores_of(load(qs_ref, tile(i)), kv_ref[positions(i), 0:HD])

    def soften(i, s_ref):
        here = tile(i)
        s, m = s_ref[...], load(m_ref, here)
        fresh = jnp.maximum(m, jnp.max(s, axis=1, keepdims=True))
        shrink = jnp.exp2(m - fresh)
        p = jnp.exp2(s - jnp.concatenate([fresh] * (BLOCK // HD), axis=1)).astype(jnp.bfloat16)
        pv = jnp.dot(p, with_ones(kv_ref[positions(i), HD:]), preferred_element_type=jnp.float32)
        save(m_ref, here, fresh)
        save(l_ref, here, load(l_ref, here) * shrink + pv[:, HD:])
        save(a_ref, here, load(a_ref, here) * shrink + pv[:, :HD])

    @pl.when(items > 0)
    def _():
        score(0, s0_ref)

    def pair(j, c):
        i = j * 2
        score(i + 1, s1_ref)
        soften(i, s0_ref)
        score(i + 2, s0_ref)
        soften(i + 1, s1_ref)
        return c

    lax.fori_loop(0, (items - 1) // 2, pair, 0)

    @pl.when((items > 0) & (items % 2 == 0))
    def _():
        score(items - 1, s1_ref)
        soften(items - 2, s0_ref)
        soften(items - 1, s1_ref)

    @pl.when(items % 2 == 1)
    def _():
        soften(items - 1, s0_ref)

    if number == 3:
        far_ref, far_stat_ref = refs[9:11]
        lane = lax.broadcasted_iota(jnp.int32, (GROUP, 128), 1)
        for g in range(16):
            to = slice(g * GROUP, (g + 1) * GROUP)
            stats = jnp.zeros((GROUP, 128), jnp.float32)
            for h in range(HEADS):
                here = slice(((16 + g) * HEADS + h) * GROUP, ((16 + g) * HEADS + h + 1) * GROUP)
                stats = put_stats(lane, stats, h, m_ref[here, :], l_ref[here, :])
                far_ref[to, h * HD : (h + 1) * HD] = a_ref[here, :].astype(jnp.bfloat16)
            far_stat_ref[to, :] = stats


def fold_call(number, plan, qs, kv, state):
    f32, b16 = jnp.float32, jnp.bfloat16
    shapes = [((STATE_ROWS, HD), f32)] * 3
    if number == 3:
        shapes += [((256, 1024), b16), ((256, 128), f32)]
    operands = [plan, qs, kv, *state]
    wide = (TILE * GROUP * HEADS, BLOCK)
    return pl.pallas_call(
        functools.partial(fold_kernel, number),
        out_shape=[jax.ShapeDtypeStruct(s, d) for s, d in shapes],
        in_specs=[SMEM] + [VMEM] * (len(operands) - 1),
        out_specs=[VMEM] * len(shapes),
        scratch_shapes=[pltpu.SMEM((48,), jnp.int32)] * 2 + [pltpu.VMEM(wide, f32)] * 2,
        input_output_aliases={3: 0, 4: 1, 5: 2},
        compiler_params=pltpu.CompilerParams(vmem_limit_bytes=40 * 2**20),
        cost_estimate=pl.CostEstimate(
            flops=2 * 2560 * kv.shape[0] * 256, bytes_accessed=4 * 2**20, transcendentals=1280 * kv.shape[0]
        ),
        name=f"fold{number}",
    )(*operands)


def join_kernel(len_ref, m_ref, l_ref, a_ref, far_ref, far_stat_ref, out_ref):
    for b in range(2):
        for part in range(2):
            length = len_ref[b] - part * 4 * GROUP
            first = b * BROWS + part * 4 * GROUP

            @pl.when(length > 0)
            def _(b=b, part=part, length=length, first=first):
                for g in range(4):
                    group = b * 8 + part * 4 + g
                    rows = slice(group * GROUP, (group + 1) * GROUP)
                    live = lax.broadcasted_iota(jnp.int32, (GROUP, HD), 0) < length - g * GROUP
                    stats = far_stat_ref[rows, :]
                    for h in range(HEADS):
                        cols = slice(h * HD, (h + 1) * HD)
                        here = slice((group * HEADS + h) * GROUP, (group * HEADS + h + 1) * GROUP)
                        m, far_m = m_ref[here, :], stats[:, h : h + 1]
                        peak = jnp.maximum(m, far_m)
                        w, far_w = jnp.exp2(m - peak), jnp.exp2(far_m - peak)
                        total = w * l_ref[here, :] + far_w * stats[:, HEADS + h : HEADS + h + 1]
                        blended = w * a_ref[here, :] + far_w * far_ref[rows, cols].astype(jnp.float32)
                        out_ref[rows, cols] = jnp.where(live, blended / total, 0.0).astype(jnp.bfloat16)

            @pl.when(length <= 0)
            def _(first=first):
                out_ref[first : first + 4 * GROUP, :] = jnp.zeros((4 * GROUP, HEADS * HD), jnp.bfloat16)


def join(lengths, state, far, far_stat):
    return pl.pallas_call(
        join_kernel,
        out_shape=jax.ShapeDtypeStruct((256, 1024), jnp.bfloat16),
        in_specs=[SMEM] + [VMEM] * 5,
        out_specs=VMEM,
        compiler_params=pltpu.CompilerParams(vmem_limit_bytes=32 * 2**20),
        name="join",
    )(lengths, *state, far, far_stat)


def per_device(queries, answer_kv, prompt_kv, block_prompt, answer_len):
    piece = prompt_kv[0, :, 0, :]
    own_kv = answer_kv[:, 0, :]
    code = block_prompt[:, 0] * 256 + answer_len
    place = jnp.stack([lax.axis_index("grp"), lax.axis_index("ctx") & 1]).astype(jnp.int32)

    even, odd, across = [lax.ppermute(piece, AXES, ring_swap(0, turn)) for turn in ("even", "odd", "across")]
    code_far, q_far = [lax.ppermute(v, AXES, core_swap()) for v in (code, queries)]
    room = jnp.pad(piece, ((0, piece.shape[0]), (0, 0)))
    plan, qs, *state = prep(jnp.concatenate([code, code_far, place]), queries, q_far, own_kv)
    even, odd, across, room, plan, qs, state = lax.optimization_barrier((even, odd, across, room, plan, qs, state))
    held = [lax.dynamic_update_slice(room, even, (piece.shape[0], 0)), jnp.concatenate([odd, across], axis=0)]
    even0, even1 = [lax.ppermute(h, AXES, ring_swap(1, "even")) for h in held]
    odd0, odd1 = [lax.ppermute(h, AXES, ring_swap(1, "odd")) for h in held]
    all_held = jnp.concatenate(held, axis=0)
    across = lax.ppermute(all_held, AXES, ring_swap(1, "across"))
    state = fold_call(0, plan, qs, all_held, state)
    even0, odd1, state = lax.optimization_barrier((even0, odd1, state))
    state = fold_call(1, plan, qs, jnp.concatenate([even0, odd1], axis=0), state)
    odd0, even1, state = lax.optimization_barrier((odd0, even1, state))
    state = fold_call(2, plan, qs, jnp.concatenate([odd0, even1], axis=0), state)
    across, state = lax.optimization_barrier((across, state))
    *state, far, far_stat = fold_call(3, plan, qs, across, state)
    far = lax.ppermute(far, AXES, core_swap())
    far_stat = lax.ppermute(far_stat, AXES, core_swap())
    state = fold_call(4, plan, qs, across, state)
    return join(answer_len, state, far, far_stat)


def solution(mesh):
    placed = (
        P(("ctx", "grp"), "head"),
        P(("ctx", "grp"), "head", None),
        P("grp", "ctx", "head", None),
        P(("ctx", "grp"), None),
        P(("ctx", "grp")),
    )
    return jax.shard_map(
        per_device, mesh=mesh, in_specs=placed, out_specs=P(("ctx", "grp"), "head"), check_vma=False
    )
```

```python
import functools

import jax
import jax.numpy as jnp
import numpy as np
from jax import lax
from jax.experimental import pallas as pl
from jax.experimental.pallas import tpu as pltpu
from jax.sharding import PartitionSpec as P

HD = 128
BROWS = 128
HEADS = 8
BLOCK = 1024
GROUP = 16
TILE = 4
LIST = 8
SPARE = 32
STATE_ROWS = 33 * GROUP * HEADS
SCALE = float(np.log2(np.e) / np.sqrt(HD))
LOW = -1e30
VMEM = pl.BlockSpec(memory_space=pltpu.VMEM)
SMEM = pl.BlockSpec(memory_space=pltpu.SMEM)
AXES = ("ctx", "grp")

TURNS = {"even": lambda i: i ^ 1, "odd": lambda i: 3 - i, "across": lambda i: i ^ 2}


def index_of(x, y, core):
    return ((y * 2 + x % 2) * 2 + core) * 2 + x // 2


def ring_swap(stage, turn):
    pairs = []
    for x in range(4):
        for y in range(4):
            for core in range(2):
                to = (TURNS[turn](x), y) if core == stage else (x, TURNS[turn](y))
                pairs.append((index_of(x, y, core), index_of(*to, core)))
    return pairs


def core_swap():
    return [(index_of(x, y, c), index_of(x, y, 1 - c)) for x in range(4) for y in range(4) for c in range(2)]


def scaled(q):
    wide = q.astype(jnp.float32) * SCALE
    high = wide.astype(jnp.bfloat16)
    low = (wide - high.astype(jnp.float32)).astype(jnp.bfloat16)
    return jnp.concatenate([high, low], axis=1)


def scores_of(q, k):
    return lax.dot_general(
        q, jnp.concatenate([k, k], axis=1), (((1,), (1,)), ((), ())), preferred_element_type=jnp.float32
    )


def with_ones(v):
    return jnp.concatenate([v, jnp.ones_like(v)], axis=1)


def put_stats(lane, stats, h, m, l):
    stats = jnp.where(lane == h, m, stats)
    return jnp.where(lane == HEADS + h, l, stats)


def make_plan(meta_ref, plan_ref):
    offset = jnp.int32(0)
    for want in range(2):
        count = jnp.int32(0)
        for b in (2, 3, 0, 1):
            code = meta_ref[b]
            live = ((code & 255) + (GROUP - 1)) // GROUP
            live = jnp.where((code >> 8) == (meta_ref[4] ^ want), live, 0)

            def add(i, c, b=b, at=LIST + offset + count):
                plan_ref[at + i] = b * 8 + i
                return c

            lax.fori_loop(0, live, add, 0)
            count = count + live
            if b == 3:
                plan_ref[3 + want] = (count + (TILE - 1)) // TILE
        tiles = (count + (TILE - 1)) // TILE
        for i in range(TILE - 1):
            plan_ref[LIST + offset + count + i] = SPARE
        plan_ref[want] = tiles
        offset = offset + tiles * TILE
    plan_ref[2] = meta_ref[5]


def rows_of(group):
    return pl.ds(pl.multiple_of(group * (GROUP * HEADS), GROUP * HEADS), GROUP * HEADS)


def prep_kernel(meta_ref, q_ref, far_ref, kv_ref, plan_ref, qs_ref, m_ref, l_ref, a_ref):
    make_plan(meta_ref, plan_ref)
    shape = (HEADS * BROWS, BROWS)
    row = lax.broadcasted_iota(jnp.int32, shape, 0) % BROWS
    causal = row >= lax.broadcasted_iota(jnp.int32, shape, 1)
    for b in range(2):
        rows = slice(b * BROWS, (b + 1) * BROWS)
        q = scaled(jnp.concatenate([q_ref[rows, h * HD : (h + 1) * HD] for h in range(HEADS)], axis=0))
        s = jnp.where(causal, scores_of(q, kv_ref[rows, 0:HD]), LOW)
        m = jnp.max(s, axis=1, keepdims=True)
        p = jnp.exp2(s - m)
        pv = jnp.dot(p.astype(jnp.bfloat16), with_ones(kv_ref[rows, HD:]), preferred_element_type=jnp.float32)
        m = jnp.broadcast_to(m, (HEADS * BROWS, HD))
        for g in range(8):
            for h in range(HEADS):
                here = slice(((b * 8 + g) * HEADS + h) * GROUP, ((b * 8 + g) * HEADS + h + 1) * GROUP)
                part = slice(h * BROWS + g * GROUP, h * BROWS + (g + 1) * GROUP)
                qs_ref[here, :] = q[part]
                m_ref[here, :] = m[part]
                l_ref[here, :] = pv[part, HD:]
                a_ref[here, :] = pv[part, :HD]
    for g in range(16):
        for h in range(HEADS):
            here = slice(((16 + g) * HEADS + h) * GROUP, ((16 + g) * HEADS + h + 1) * GROUP)
            qs_ref[here, :] = scaled(far_ref[g * GROUP : (g + 1) * GROUP, h * HD : (h + 1) * HD])
    rest = slice(16 * GROUP * HEADS, STATE_ROWS)
    size = (STATE_ROWS - 16 * GROUP * HEADS, HD)
    m_ref[rest, :] = jnp.full(size, LOW, jnp.float32)
    l_ref[rest, :] = jnp.zeros(size, jnp.float32)
    a_ref[rest, :] = jnp.zeros(size, jnp.float32)
    qs_ref[SPARE * GROUP * HEADS : STATE_ROWS, :] = jnp.zeros((GROUP * HEADS, 2 * HD), jnp.bfloat16)


def prep(meta, q, far, kv):
    return pl.pallas_call(
        prep_kernel,
        out_shape=[
            jax.ShapeDtypeStruct((64,), jnp.int32),
            jax.ShapeDtypeStruct((STATE_ROWS, 2 * HD), jnp.bfloat16),
        ]
        + [jax.ShapeDtypeStruct((STATE_ROWS, HD), jnp.float32)] * 3,
        in_specs=[SMEM] + [VMEM] * 3,
        out_specs=[SMEM] + [VMEM] * 4,
        compiler_params=pltpu.CompilerParams(vmem_limit_bytes=40 * 2**20),
        cost_estimate=pl.CostEstimate(flops=2 * 2048 * 128 * 512, bytes_accessed=3 * 2**20, transcendentals=2048 * 128),
        name="prep",
    )(meta, q, far, kv)


def fold_kernel(number, *refs):
    refs = list(refs)
    plan_ref, qs_ref, kv_ref = refs[:3]
    m_ref, l_ref, a_ref = refs[6:9]
    item_at, item_kv, s0_ref, s1_ref = refs[-4:]
    core = plan_ref[2]

    items, first = jnp.int32(0), jnp.int32(LIST)
    for want in range(2):
        tiles, far_tiles = plan_ref[want], plan_ref[3 + want]
        start = far_tiles if number == 4 else 0
        used = (far_tiles if number == 3 else tiles) - start
        if number == 0:
            blocks, many = (0,), 1 - want
        elif number == 5:
            blocks, many = (1,), jnp.where((want ^ core) == 1, 1, 0)
        elif number == 1:
            blocks, many = (want, 0), 1
        elif number == 2:
            blocks, many = (want ^ core, 0), 1
        else:
            blocks, many = (jnp.where(core == 0, want, 0), 1), jnp.where(core == 0, 1, 2 * want)

        def add(t, c, first=first, blocks=blocks, many=many, items=items, start=start):
            for i in range(2 if number in (3, 4) else 1):

                @pl.when(i < many)
                def _(i=i):
                    item_at[items + t * many + i] = first + (start + t) * TILE
                    item_kv[items + t * many + i] = blocks[i]

            return c

        lax.fori_loop(0, used, add, 0)
        items = items + used * many
        first = first + tiles * TILE
    for i in range(2):
        item_at[items + i] = LIST
        item_kv[items + i] = 0

    def tile(i):
        return [rows_of(plan_ref[item_at[i] + g]) for g in range(TILE)]

    def positions(i):
        return pl.ds(pl.multiple_of(item_kv[i] * BLOCK, BLOCK), BLOCK)

    def load(ref, rows):
        return jnp.concatenate([ref[r, :] for r in rows], axis=0)

    def save(ref, rows, value):
        for g, r in enumerate(rows):
            ref[r, :] = value[g * GROUP * HEADS : (g + 1) * GROUP * HEADS]

    def score(i, s_ref):
        s_ref[...] = scores_of(load(qs_ref, tile(i)), kv_ref[positions(i), 0:HD])

    def soften(i, s_ref):
        here = tile(i)
        s, m = s_ref[...], load(m_ref, here)
        fresh = jnp.maximum(m, jnp.max(s, axis=1, keepdims=True))
        shrink = jnp.exp2(m - fresh)
        p = jnp.exp2(s - jnp.concatenate([fresh] * (BLOCK // HD), axis=1)).astype(jnp.bfloat16)
        pv = jnp.dot(p, with_ones(kv_ref[positions(i), HD:]), preferred_element_type=jnp.float32)
        save(m_ref, here, fresh)
        save(l_ref, here, load(l_ref, here) * shrink + pv[:, HD:])
        save(a_ref, here, load(a_ref, here) * shrink + pv[:, :HD])

    @pl.when(items > 0)
    def _():
        score(0, s0_ref)

    def pair(j, c):
        i = j * 2
        score(i + 1, s1_ref)
        soften(i, s0_ref)
        score(i + 2, s0_ref)
        soften(i + 1, s1_ref)
        return c

    lax.fori_loop(0, (items - 1) // 2, pair, 0)

    @pl.when((items > 0) & (items % 2 == 0))
    def _():
        score(items - 1, s1_ref)
        soften(items - 2, s0_ref)
        soften(items - 1, s1_ref)

    @pl.when(items % 2 == 1)
    def _():
        soften(items - 1, s0_ref)

    if number == 3:
        far_ref, far_stat_ref = refs[9:11]
        lane = lax.broadcasted_iota(jnp.int32, (GROUP, 128), 1)
        for g in range(16):
            to = slice(g * GROUP, (g + 1) * GROUP)
            stats = jnp.zeros((GROUP, 128), jnp.float32)
            for h in range(HEADS):
                here = slice(((16 + g) * HEADS + h) * GROUP, ((16 + g) * HEADS + h + 1) * GROUP)
                stats = put_stats(lane, stats, h, m_ref[here, :], l_ref[here, :])
                far_ref[to, h * HD : (h + 1) * HD] = a_ref[here, :].astype(jnp.bfloat16)
            far_stat_ref[to, :] = stats


def fold_call(number, plan, qs, kv, state):
    f32, b16 = jnp.float32, jnp.bfloat16
    shapes = [((STATE_ROWS, HD), f32)] * 3
    if number == 3:
        shapes += [((256, 1024), b16), ((256, 128), f32)]
    operands = [plan, qs, kv, *state]
    wide = (TILE * GROUP * HEADS, BLOCK)
    return pl.pallas_call(
        functools.partial(fold_kernel, number),
        out_shape=[jax.ShapeDtypeStruct(s, d) for s, d in shapes],
        in_specs=[SMEM] + [VMEM] * (len(operands) - 1),
        out_specs=[VMEM] * len(shapes),
        scratch_shapes=[pltpu.SMEM((48,), jnp.int32)] * 2 + [pltpu.VMEM(wide, f32)] * 2,
        input_output_aliases={3: 0, 4: 1, 5: 2},
        compiler_params=pltpu.CompilerParams(vmem_limit_bytes=40 * 2**20),
        cost_estimate=pl.CostEstimate(
            flops=2 * 2560 * kv.shape[0] * 256, bytes_accessed=4 * 2**20, transcendentals=1280 * kv.shape[0]
        ),
        name=f"fold{number}",
    )(*operands)


def join_kernel(len_ref, m_ref, l_ref, a_ref, far_ref, far_stat_ref, out_ref):
    for b in range(2):
        for part in range(2):
            length = len_ref[b] - part * 4 * GROUP
            first = b * BROWS + part * 4 * GROUP

            @pl.when(length > 0)
            def _(b=b, part=part, length=length, first=first):
                for g in range(4):
                    group = b * 8 + part * 4 + g
                    rows = slice(group * GROUP, (group + 1) * GROUP)
                    live = lax.broadcasted_iota(jnp.int32, (GROUP, HD), 0) < length - g * GROUP
                    stats = far_stat_ref[rows, :]
                    for h in range(HEADS):
                        cols = slice(h * HD, (h + 1) * HD)
                        here = slice((group * HEADS + h) * GROUP, (group * HEADS + h + 1) * GROUP)
                        m, far_m = m_ref[here, :], stats[:, h : h + 1]
                        peak = jnp.maximum(m, far_m)
                        w, far_w = jnp.exp2(m - peak), jnp.exp2(far_m - peak)
                        total = w * l_ref[here, :] + far_w * stats[:, HEADS + h : HEADS + h + 1]
                        blended = w * a_ref[here, :] + far_w * far_ref[rows, cols].astype(jnp.float32)
                        out_ref[rows, cols] = jnp.where(live, blended / total, 0.0).astype(jnp.bfloat16)

            @pl.when(length <= 0)
            def _(first=first):
                out_ref[first : first + 4 * GROUP, :] = jnp.zeros((4 * GROUP, HEADS * HD), jnp.bfloat16)


def join(lengths, state, far, far_stat):
    return pl.pallas_call(
        join_kernel,
        out_shape=jax.ShapeDtypeStruct((256, 1024), jnp.bfloat16),
        in_specs=[SMEM] + [VMEM] * 5,
        out_specs=VMEM,
        compiler_params=pltpu.CompilerParams(vmem_limit_bytes=32 * 2**20),
        name="join",
    )(lengths, *state, far, far_stat)


def per_device(queries, answer_kv, prompt_kv, block_prompt, answer_len):
    piece = prompt_kv[0, :, 0, :]
    own_kv = answer_kv[:, 0, :]
    code = block_prompt[:, 0] * 256 + answer_len
    place = jnp.stack([lax.axis_index("grp"), lax.axis_index("ctx") & 1]).astype(jnp.int32)

    even, odd, across = [lax.ppermute(piece, AXES, ring_swap(0, turn)) for turn in ("even", "odd", "across")]
    code_far, q_far = [lax.ppermute(v, AXES, core_swap()) for v in (code, queries)]
    room = jnp.pad(piece, ((0, piece.shape[0]), (0, 0)))
    plan, qs, *state = prep(jnp.concatenate([code, code_far, place]), queries, q_far, own_kv)
    even, odd, across, room, plan, qs, state = lax.optimization_barrier((even, odd, across, room, plan, qs, state))
    held = [lax.dynamic_update_slice(room, even, (piece.shape[0], 0)), jnp.concatenate([odd, across], axis=0)]
    even0, even1 = [lax.ppermute(h, AXES, ring_swap(1, "even")) for h in held]
    odd0, odd1 = [lax.ppermute(h, AXES, ring_swap(1, "odd")) for h in held]
    all_held = jnp.concatenate(held, axis=0)
    state = fold_call(0, plan, qs, all_held, state)
    even0, odd1, state = lax.optimization_barrier((even0, odd1, state))
    last = [
        lax.ppermute(even0, AXES, ring_swap(1, "odd")),
        lax.ppermute(odd1, AXES, ring_swap(1, "even")),
    ]
    state = fold_call(5, plan, qs, all_held, state)
    state = fold_call(1, plan, qs, jnp.concatenate([even0, odd1], axis=0), state)
    odd0, even1, state = lax.optimization_barrier((odd0, even1, state))
    state = fold_call(2, plan, qs, jnp.concatenate([odd0, even1], axis=0), state)
    last, state = lax.optimization_barrier((last, state))
    across = jnp.concatenate(last, axis=0)
    *state, far, far_stat = fold_call(3, plan, qs, across, state)
    far = lax.ppermute(far, AXES, core_swap())
    far_stat = lax.ppermute(far_stat, AXES, core_swap())
    state = fold_call(4, plan, qs, across, state)
    return join(answer_len, state, far, far_stat)


def solution(mesh):
    placed = (
        P(("ctx", "grp"), "head"),
        P(("ctx", "grp"), "head", None),
        P("grp", "ctx", "head", None),
        P(("ctx", "grp"), None),
        P(("ctx", "grp")),
    )
    return jax.shard_map(
        per_device, mesh=mesh, in_specs=placed, out_specs=P(("ctx", "grp"), "head"), check_vma=False
    )
```

```python
import functools

import jax
import jax.numpy as jnp
import numpy as np
from jax import lax
from jax.experimental import pallas as pl
from jax.experimental.pallas import tpu as pltpu
from jax.sharding import PartitionSpec as P

HD = 128
BROWS = 128
HEADS = 8
BLOCK = 1024
GROUP = 16
TILE = 4
LIST = 8
SPARE = 32
STATE_ROWS = 33 * GROUP * HEADS
SCALE = float(np.log2(np.e) / np.sqrt(HD))
LOW = -1e30
VMEM = pl.BlockSpec(memory_space=pltpu.VMEM)
SMEM = pl.BlockSpec(memory_space=pltpu.SMEM)
AXES = ("ctx", "grp")

TURNS = {"even": lambda i: i ^ 1, "odd": lambda i: 3 - i, "across": lambda i: i ^ 2}


def index_of(x, y, core):
    return ((y * 2 + x % 2) * 2 + core) * 2 + x // 2


def ring_swap(stage, turn):
    pairs = []
    for x in range(4):
        for y in range(4):
            for core in range(2):
                to = (TURNS[turn](x), y) if core == stage else (x, TURNS[turn](y))
                pairs.append((index_of(x, y, core), index_of(*to, core)))
    return pairs


def core_swap():
    return [(index_of(x, y, c), index_of(x, y, 1 - c)) for x in range(4) for y in range(4) for c in range(2)]


def scaled(q):
    wide = q.astype(jnp.float32) * SCALE
    high = wide.astype(jnp.bfloat16)
    low = (wide - high.astype(jnp.float32)).astype(jnp.bfloat16)
    return jnp.concatenate([high, low], axis=1)


def scores_of(q, k):
    return lax.dot_general(
        q, jnp.concatenate([k, k], axis=1), (((1,), (1,)), ((), ())), preferred_element_type=jnp.float32
    )


def with_ones(v):
    return jnp.concatenate([v, jnp.ones_like(v)], axis=1)


def put_stats(lane, stats, h, m, l):
    stats = jnp.where(lane == h, m, stats)
    return jnp.where(lane == HEADS + h, l, stats)


def make_plan(meta_ref, plan_ref):
    offset = jnp.int32(0)
    for want in range(2):
        count = jnp.int32(0)
        for b in (2, 3, 0, 1):
            code = meta_ref[b]
            live = ((code & 255) + (GROUP - 1)) // GROUP
            live = jnp.where((code >> 8) == (meta_ref[4] ^ want), live, 0)

            def add(i, c, b=b, at=LIST + offset + count):
                plan_ref[at + i] = b * 8 + i
                return c

            lax.fori_loop(0, live, add, 0)
            count = count + live
            if b == 3:
                far_tiles = (count + (TILE - 1)) // TILE
        tiles = (count + (TILE - 1)) // TILE
        for i in range(TILE - 1):
            plan_ref[LIST + offset + count + i] = SPARE
        plan_ref[want] = tiles
        plan_ref[3 + want] = jnp.maximum(far_tiles, tiles - far_tiles)
        offset = offset + tiles * TILE
    plan_ref[2] = meta_ref[5]


def rows_of(group):
    return pl.ds(pl.multiple_of(group * (GROUP * HEADS), GROUP * HEADS), GROUP * HEADS)


def prep_kernel(meta_ref, q_ref, far_ref, kv_ref, plan_ref, qs_ref, m_ref, l_ref, a_ref):
    make_plan(meta_ref, plan_ref)
    shape = (HEADS * BROWS, BROWS)
    row = lax.broadcasted_iota(jnp.int32, shape, 0) % BROWS
    causal = row >= lax.broadcasted_iota(jnp.int32, shape, 1)
    for b in range(2):
        rows = slice(b * BROWS, (b + 1) * BROWS)
        q = scaled(jnp.concatenate([q_ref[rows, h * HD : (h + 1) * HD] for h in range(HEADS)], axis=0))
        s = jnp.where(causal, scores_of(q, kv_ref[rows, 0:HD]), LOW)
        m = jnp.max(s, axis=1, keepdims=True)
        p = jnp.exp2(s - m)
        pv = jnp.dot(p.astype(jnp.bfloat16), with_ones(kv_ref[rows, HD:]), preferred_element_type=jnp.float32)
        m = jnp.broadcast_to(m, (HEADS * BROWS, HD))
        for g in range(8):
            for h in range(HEADS):
                here = slice(((b * 8 + g) * HEADS + h) * GROUP, ((b * 8 + g) * HEADS + h + 1) * GROUP)
                part = slice(h * BROWS + g * GROUP, h * BROWS + (g + 1) * GROUP)
                qs_ref[here, :] = q[part]
                m_ref[here, :] = m[part]
                l_ref[here, :] = pv[part, HD:]
                a_ref[here, :] = pv[part, :HD]
    for g in range(16):
        for h in range(HEADS):
            here = slice(((16 + g) * HEADS + h) * GROUP, ((16 + g) * HEADS + h + 1) * GROUP)
            qs_ref[here, :] = scaled(far_ref[g * GROUP : (g + 1) * GROUP, h * HD : (h + 1) * HD])
    rest = slice(16 * GROUP * HEADS, STATE_ROWS)
    size = (STATE_ROWS - 16 * GROUP * HEADS, HD)
    m_ref[rest, :] = jnp.full(size, LOW, jnp.float32)
    l_ref[rest, :] = jnp.zeros(size, jnp.float32)
    a_ref[rest, :] = jnp.zeros(size, jnp.float32)
    qs_ref[SPARE * GROUP * HEADS : STATE_ROWS, :] = jnp.zeros((GROUP * HEADS, 2 * HD), jnp.bfloat16)


def prep(meta, q, far, kv):
    return pl.pallas_call(
        prep_kernel,
        out_shape=[
            jax.ShapeDtypeStruct((64,), jnp.int32),
            jax.ShapeDtypeStruct((STATE_ROWS, 2 * HD), jnp.bfloat16),
        ]
        + [jax.ShapeDtypeStruct((STATE_ROWS, HD), jnp.float32)] * 3,
        in_specs=[SMEM] + [VMEM] * 3,
        out_specs=[SMEM] + [VMEM] * 4,
        compiler_params=pltpu.CompilerParams(vmem_limit_bytes=40 * 2**20),
        cost_estimate=pl.CostEstimate(flops=2 * 2048 * 128 * 512, bytes_accessed=3 * 2**20, transcendentals=2048 * 128),
        name="prep",
    )(meta, q, far, kv)


def fold_kernel(number, *refs):
    refs = list(refs)
    plan_ref, qs_ref, kv_ref = refs[:3]
    m_ref, l_ref, a_ref = refs[6:9]
    item_at, item_kv, s0_ref, s1_ref = refs[-4:]
    core = plan_ref[2]

    items, first = jnp.int32(0), jnp.int32(LIST)
    for want in range(2):
        tiles, far_tiles = plan_ref[want], plan_ref[3 + want]
        start = far_tiles if number == 4 else 0
        used = (far_tiles if number == 3 else tiles) - start
        if number == 1:
            blocks, many = (want, 0), 1
        elif number == 2:
            blocks, many = (want ^ core, 0), 1
        else:
            blocks = (jnp.where(core == 0, want, 0), 1)
            many = jnp.where(core == 0, 1, 2 if (want == 0) == (number == 0) else 0)

        def add(t, c, first=first, blocks=blocks, many=many, items=items, start=start):
            for i in range(1 if number in (1, 2) else 2):

                @pl.when(i < many)
                def _(i=i):
                    item_at[items + t * many + i] = first + (start + t) * TILE
                    item_kv[items + t * many + i] = blocks[i]

            return c

        lax.fori_loop(0, used, add, 0)
        items = items + used * many
        first = first + tiles * TILE
    for i in range(2):
        item_at[items + i] = LIST
        item_kv[items + i] = 0

    def tile(i):
        return [rows_of(plan_ref[item_at[i] + g]) for g in range(TILE)]

    def positions(i):
        return pl.ds(pl.multiple_of(item_kv[i] * BLOCK, BLOCK), BLOCK)

    def load(ref, rows):
        return jnp.concatenate([ref[r, :] for r in rows], axis=0)

    def save(ref, rows, value):
        for g, r in enumerate(rows):
            ref[r, :] = value[g * GROUP * HEADS : (g + 1) * GROUP * HEADS]

    def score(i, s_ref):
        s_ref[...] = scores_of(load(qs_ref, tile(i)), kv_ref[positions(i), 0:HD])

    def soften(i, s_ref):
        here = tile(i)
        s, m = s_ref[...], load(m_ref, here)
        fresh = jnp.maximum(m, jnp.max(s, axis=1, keepdims=True))
        shrink = jnp.exp2(m - fresh)
        p = jnp.exp2(s - jnp.concatenate([fresh] * (BLOCK // HD), axis=1)).astype(jnp.bfloat16)
        pv = jnp.dot(p, with_ones(kv_ref[positions(i), HD:]), preferred_element_type=jnp.float32)
        save(m_ref, here, fresh)
        save(l_ref, here, load(l_ref, here) * shrink + pv[:, HD:])
        save(a_ref, here, load(a_ref, here) * shrink + pv[:, :HD])

    @pl.when(items > 0)
    def _():
        score(0, s0_ref)

    def pair(j, c):
        i = j * 2
        score(i + 1, s1_ref)
        soften(i, s0_ref)
        score(i + 2, s0_ref)
        soften(i + 1, s1_ref)
        return c

    lax.fori_loop(0, (items - 1) // 2, pair, 0)

    @pl.when((items > 0) & (items % 2 == 0))
    def _():
        score(items - 1, s1_ref)
        soften(items - 2, s0_ref)
        soften(items - 1, s1_ref)

    @pl.when(items % 2 == 1)
    def _():
        soften(items - 1, s0_ref)

    if number == 3:
        far_ref, far_stat_ref = refs[9:11]
        lane = lax.broadcasted_iota(jnp.int32, (GROUP, 128), 1)
        for g in range(16):
            to = slice(g * GROUP, (g + 1) * GROUP)
            stats = jnp.zeros((GROUP, 128), jnp.float32)
            for h in range(HEADS):
                here = slice(((16 + g) * HEADS + h) * GROUP, ((16 + g) * HEADS + h + 1) * GROUP)
                stats = put_stats(lane, stats, h, m_ref[here, :], l_ref[here, :])
                far_ref[to, h * HD : (h + 1) * HD] = a_ref[here, :].astype(jnp.bfloat16)
            far_stat_ref[to, :] = stats


def fold_call(number, plan, qs, kv, state):
    f32, b16 = jnp.float32, jnp.bfloat16
    shapes = [((STATE_ROWS, HD), f32)] * 3
    if number == 3:
        shapes += [((256, 1024), b16), ((256, 128), f32)]
    operands = [plan, qs, kv, *state]
    wide = (TILE * GROUP * HEADS, BLOCK)
    return pl.pallas_call(
        functools.partial(fold_kernel, number),
        out_shape=[jax.ShapeDtypeStruct(s, d) for s, d in shapes],
        in_specs=[SMEM] + [VMEM] * (len(operands) - 1),
        out_specs=[VMEM] * len(shapes),
        scratch_shapes=[pltpu.SMEM((48,), jnp.int32)] * 2 + [pltpu.VMEM(wide, f32)] * 2,
        input_output_aliases={3: 0, 4: 1, 5: 2},
        compiler_params=pltpu.CompilerParams(vmem_limit_bytes=40 * 2**20),
        cost_estimate=pl.CostEstimate(
            flops=2 * 2560 * kv.shape[0] * 256, bytes_accessed=4 * 2**20, transcendentals=1280 * kv.shape[0]
        ),
        name=f"fold{number}",
    )(*operands)


def join_kernel(len_ref, m_ref, l_ref, a_ref, far_ref, far_stat_ref, out_ref):
    for b in range(2):
        for part in range(2):
            length = len_ref[b] - part * 4 * GROUP
            first = b * BROWS + part * 4 * GROUP

            @pl.when(length > 0)
            def _(b=b, part=part, length=length, first=first):
                for g in range(4):
                    group = b * 8 + part * 4 + g
                    rows = slice(group * GROUP, (group + 1) * GROUP)
                    live = lax.broadcasted_iota(jnp.int32, (GROUP, HD), 0) < length - g * GROUP
                    stats = far_stat_ref[rows, :]
                    for h in range(HEADS):
                        cols = slice(h * HD, (h + 1) * HD)
                        here = slice((group * HEADS + h) * GROUP, (group * HEADS + h + 1) * GROUP)
                        m, far_m = m_ref[here, :], stats[:, h : h + 1]
                        peak = jnp.maximum(m, far_m)
                        w, far_w = jnp.exp2(m - peak), jnp.exp2(far_m - peak)
                        total = w * l_ref[here, :] + far_w * stats[:, HEADS + h : HEADS + h + 1]
                        blended = w * a_ref[here, :] + far_w * far_ref[rows, cols].astype(jnp.float32)
                        out_ref[rows, cols] = jnp.where(live, blended / total, 0.0).astype(jnp.bfloat16)

            @pl.when(length <= 0)
            def _(first=first):
                out_ref[first : first + 4 * GROUP, :] = jnp.zeros((4 * GROUP, HEADS * HD), jnp.bfloat16)


def join(lengths, state, far, far_stat):
    return pl.pallas_call(
        join_kernel,
        out_shape=jax.ShapeDtypeStruct((256, 1024), jnp.bfloat16),
        in_specs=[SMEM] + [VMEM] * 5,
        out_specs=VMEM,
        compiler_params=pltpu.CompilerParams(vmem_limit_bytes=32 * 2**20),
        name="join",
    )(lengths, *state, far, far_stat)


def per_device(queries, answer_kv, prompt_kv, block_prompt, answer_len):
    piece = prompt_kv[0, :, 0, :]
    own_kv = answer_kv[:, 0, :]
    code = block_prompt[:, 0] * 256 + answer_len
    place = jnp.stack([lax.axis_index("grp"), lax.axis_index("ctx") & 1]).astype(jnp.int32)

    even, odd, across = [lax.ppermute(piece, AXES, ring_swap(0, turn)) for turn in ("even", "odd", "across")]
    code_far, q_far = [lax.ppermute(v, AXES, core_swap()) for v in (code, queries)]
    room = jnp.pad(piece, ((0, piece.shape[0]), (0, 0)))
    plan, qs, *state = prep(jnp.concatenate([code, code_far, place]), queries, q_far, own_kv)
    even, odd, across, room, plan, qs, state = lax.optimization_barrier((even, odd, across, room, plan, qs, state))
    held = [lax.dynamic_update_slice(room, even, (piece.shape[0], 0)), jnp.concatenate([odd, across], axis=0)]
    even0, even1 = [lax.ppermute(h, AXES, ring_swap(1, "even")) for h in held]
    odd0, odd1 = [lax.ppermute(h, AXES, ring_swap(1, "odd")) for h in held]
    all_held = jnp.concatenate(held, axis=0)
    across = lax.ppermute(all_held, AXES, ring_swap(1, "across"))
    state = fold_call(0, plan, qs, all_held, state)
    even0, odd1, state = lax.optimization_barrier((even0, odd1, state))
    state = fold_call(1, plan, qs, jnp.concatenate([even0, odd1], axis=0), state)
    odd0, even1, state = lax.optimization_barrier((odd0, even1, state))
    state = fold_call(2, plan, qs, jnp.concatenate([odd0, even1], axis=0), state)
    across, state = lax.optimization_barrier((across, state))
    *state, far, far_stat = fold_call(3, plan, qs, across, state)
    far = lax.ppermute(far, AXES, core_swap())
    far_stat = lax.ppermute(far_stat, AXES, core_swap())
    state = fold_call(4, plan, qs, across, state)
    return join(answer_len, state, far, far_stat)


def solution(mesh):
    placed = (
        P(("ctx", "grp"), "head"),
        P(("ctx", "grp"), "head", None),
        P("grp", "ctx", "head", None),
        P(("ctx", "grp"), None),
        P(("ctx", "grp")),
    )
    return jax.shard_map(
        per_device, mesh=mesh, in_specs=placed, out_specs=P(("ctx", "grp"), "head"), check_vma=False
    )
```
